256 devices in a mesh: tm: 32 (over x, z), tensor: 4 (over y), dp: 2 (over core).
Axes of the slice: x: 4, y: 4, z: 8, core: 2. Of those that a mesh axis runs over, the one named last changes fastest.
Arguments:
- query_rows: bfloat16 [2, 4096, 1024], P('dp', 'tm', 'tensor'), may hold values from -8 to 8
- key_rows: bfloat16 [2, 4096, 1024], P('dp', 'tm', 'tensor'), may hold values from -8 to 8
- value_rows: bfloat16 [2, 4096, 1024], P('dp', 'tm', 'tensor'), may hold values from -6 to 6
- out_weight: bfloat16 [1024, 2048], P('tensor'), may hold values from -0.1875 to 0.1875
- cotangent: bfloat16 [2, 4096, 2048], P('dp', ('tm', 'tensor')), may hold values from -6 to 6
- tile_mask: int32 [32, 32], replicated, may hold values from 0 to 1, as said below
Outputs:
- mixed: bfloat16 [2, 4096, 2048], P('dp', ('tm', 'tensor'))
- grad_queries: bfloat16 [2, 4096, 1024], P('dp', 'tm', 'tensor')
- grad_keys: bfloat16 [2, 4096, 1024], P('dp', 'tm', 'tensor')
- grad_values: bfloat16 [2, 4096, 1024], P('dp', 'tm', 'tensor')
- grad_weight: float32 [1024, 2048], P('tensor')
The draws below stay inside these ranges and needn't reach their ends.
Inputs may be any that keep to these rules, and one draw needn't show every extreme that they name: tile_mask[i, j] is 1 exactly when the sweep of tile j (tile index // 2) is not later than that of tile i and the places of the two tiles within their sweeps (tile index % 2) differ by at most a radius of tile i, which lies in 0 to 3; tile_mask[i, i] is 1.
All inputs are finite; a program needn't handle non-finite values.
Results may differ from the reference program's by a relative error of at most 0.03.
Values may be sent and summed in bfloat16 or wider, within the bound.
No kernel may reach another device: no remote copies, remote signals or barrier semaphores. Data moves between devices by JAX's collectives and lax.ppermute only.
A program may use at most 64 MiB of HBM per device.

```python
import jax
import jax.numpy as jnp
from jax import lax

D = 2048
HD = 128
H_WIN = 8
TILE = 128
TOK_DEV = 128
QW = 1024
TOKENS = 4096
WINDOWS = 2
TILES = 32


def draw_query_rows(key, part):
    key = jax.random.fold_in(key, 1)
    base = jnp.clip(1.5 * jax.random.normal(key, (WINDOWS, TOKENS, QW), jnp.float32), -8.0, 8.0)
    return base.astype(jnp.bfloat16)


def draw_key_rows(key, part):
    key = jax.random.fold_in(key, 2)
    base = jnp.clip(1.5 * jax.random.normal(key, (WINDOWS, TOKENS, QW), jnp.float32), -8.0, 8.0)
    return base.astype(jnp.bfloat16)


def draw_tile_mask(key, part):
    key = jax.random.fold_in(key, 3)
    per_sweep = 2 * TOK_DEV // TILE
    radius = jax.random.randint(key, (TILES,), 0, 4)
    index = jnp.arange(TILES)
    sweep = index // per_sweep
    spot = index % per_sweep
    earlier = sweep[None, :] <= sweep[:, None]
    nearby = jnp.abs(spot[None, :] - spot[:, None]) <= radius[:, None]
    return (earlier & nearby).astype(jnp.int32)


def block_scale(own_key, extent, cuts, least, largest):
    loudness = 1.0
    for position, shards_of in cuts:
        heights = jax.random.uniform(jax.random.fold_in(jax.random.fold_in(own_key, 6), position), (shards_of,), jnp.float32, least / len(cuts), largest / len(cuts))
        loudness = loudness * jnp.repeat(jnp.exp(heights), extent[position] // shards_of).reshape((-1,) + (1,) * (len(extent) - 1 - position))
    return loudness


def scatter_about(rng, shape, scale, limit, cuts=(), kind=jnp.bfloat16):
    entries = jax.random.normal(rng, shape, jnp.float32) * scale
    if len(cuts) > 0:
        entries = block_scale(rng, shape, cuts, -0.22, 0.18) * entries
    return jnp.clip(entries, min=-limit, max=limit).astype(kind)


def setup_inputs(seed: int = 0) -> dict:
    streams_of = jax.random.split(jax.random.key(seed), 7)
    query_rows = draw_query_rows(jax.random.fold_in(streams_of[6], 71), 0)
    key_rows = draw_key_rows(jax.random.fold_in(streams_of[6], 71), 0)
    value_rows = scatter_about(streams_of[2], (WINDOWS, TOKENS, QW), 1.0, 6.0, ((0, 2), (1, 32), (2, 4)))
    out_weight = scatter_about(streams_of[3], (QW, D), QW ** -0.5, 0.1875, ((0, 4),))
    cotangent = scatter_about(streams_of[4], (WINDOWS, TOKENS, D), 1.0, 6.0, ((0, 2), (1, 128)))
    tile_mask = draw_tile_mask(jax.random.fold_in(streams_of[6], 71), 0)
    return {"query_rows": query_rows, "key_rows": key_rows, "value_rows": value_rows, "out_weight": out_weight, "cotangent": cotangent, "tile_mask": tile_mask}


def expand_mask(tile_mask):
    return jnp.repeat(jnp.repeat(tile_mask > 0, TILE, axis=0), TILE, axis=1)


def by_heads(matrix):
    return matrix.reshape(TOKENS, H_WIN, HD).transpose(1, 0, 2)


def from_heads(stacked):
    return stacked.transpose(1, 0, 2).reshape(TOKENS, QW)


def reference(query_rows, key_rows, value_rows, out_weight, cotangent, tile_mask):
    allowed = expand_mask(tile_mask)
    scaling = HD ** -0.5

    def forward_head(inputs):
        query_head, key_head, value_head = inputs
        scores = jnp.dot(query_head, key_head.T, preferred_element_type=jnp.float32) * scaling
        scores = jnp.where(allowed, scores, -1e30)
        row_max = jnp.max(scores, axis=1)
        weights = jnp.where(allowed, jnp.exp(scores - row_max[:, None]), 0.0)
        totals = jnp.sum(weights, axis=1)
        attended = jnp.dot(weights.astype(jnp.bfloat16), value_head, preferred_element_type=jnp.float32) / totals[:, None]
        return attended, row_max + jnp.log(totals)

    def backward_head(inputs):
        query_head, key_head, value_head, grad_head, lse_head, delta_head = inputs
        scores = jnp.dot(query_head, key_head.T, preferred_element_type=jnp.float32) * scaling
        probs = jnp.where(allowed, jnp.exp(jnp.where(allowed, scores, -1e30) - lse_head[:, None]), 0.0)
        grad_value = jnp.dot(probs.astype(jnp.bfloat16).T, grad_head, preferred_element_type=jnp.float32)
        grad_probs = jnp.dot(grad_head, value_head.T, preferred_element_type=jnp.float32)
        grad_scores = (probs * (grad_probs - delta_head[:, None])).astype(jnp.bfloat16)
        grad_query = jnp.dot(grad_scores, key_head, preferred_element_type=jnp.float32) * scaling
        grad_key = jnp.dot(grad_scores.T, query_head, preferred_element_type=jnp.float32) * scaling
        return grad_query, grad_key, grad_value

    mixed_list, grad_q_list, grad_k_list, grad_v_list = [], [], [], []
    grad_weight = jnp.zeros((QW, D), jnp.float32)
    for window in range(WINDOWS):
        query_heads = by_heads(query_rows[window])
        key_heads = by_heads(key_rows[window])
        value_heads = by_heads(value_rows[window])
        attended_heads, lse = lax.map(forward_head, (query_heads, key_heads, value_heads))
        attended = from_heads(attended_heads).astype(jnp.bfloat16)
        mixed_list.append(jnp.dot(attended, out_weight, preferred_element_type=jnp.float32).astype(jnp.bfloat16))
        grad_attended = jnp.dot(cotangent[window], out_weight.T, preferred_element_type=jnp.float32).astype(jnp.bfloat16)
        grad_weight = grad_weight + jnp.dot(attended.T, cotangent[window], preferred_element_type=jnp.float32)
        delta = (grad_attended.astype(jnp.float32) * attended.astype(jnp.float32)).reshape(TOKENS, H_WIN, HD).sum(axis=2).T
        grad_q, grad_k, grad_v = lax.map(backward_head, (query_heads, key_heads, value_heads, by_heads(grad_attended), lse, delta))
        grad_q_list.append(from_heads(grad_q).astype(jnp.bfloat16))
        grad_k_list.append(from_heads(grad_k).astype(jnp.bfloat16))
        grad_v_list.append(from_heads(grad_v).astype(jnp.bfloat16))
    return (jnp.stack(mixed_list), jnp.stack(grad_q_list), jnp.stack(grad_k_list), jnp.stack(grad_v_list), grad_weight)
```

```python
import functools
import math

import jax
import jax.numpy as jnp
from jax import lax
from jax.experimental import pallas as pl
from jax.experimental.pallas import tpu as pltpu
from jax.sharding import PartitionSpec as P

HD = 128
TILE = 128
BLK = 256
SCALE = HD ** (-0.5)
LOG2E = math.log2(math.e)
LOW = -1e30
F32 = jnp.float32
BF16 = jnp.bfloat16
X, ZH, PAR, Y = 0, 1, 2, 3
NN = (((1,), (0,)), ((), ()))
NT = (((1,), (1,)), ((), ()))


def dot(a, b, dims=NN):
    return lax.dot_general(a, b, dims, preferred_element_type=F32)


def call(body, outs, ins, flops=0, scratch=(), smem=1, vmem=48):
    specs = [pl.BlockSpec(memory_space=pltpu.SMEM)] * smem
    specs += [pl.BlockSpec(memory_space=pltpu.VMEM)] * (len(ins) - smem)
    shapes = [jax.ShapeDtypeStruct(s, d) for s, d in outs]
    moved = sum(math.prod(a.shape) * a.dtype.itemsize for a in list(ins) + shapes)
    return pl.pallas_call(
        body,
        out_shape=shapes,
        in_specs=specs,
        out_specs=[pl.BlockSpec(memory_space=pltpu.VMEM)] * len(outs),
        scratch_shapes=list(scratch),
        compiler_params=pltpu.CompilerParams(vmem_limit_bytes=vmem * 2**20),
        cost_estimate=pl.CostEstimate(flops=flops, bytes_accessed=moved, transcendentals=0),
    )(*ins)


def split_heads(pos, q, k, v, keep, send):
    for n, ref in enumerate((q, k, v)):
        rows = slice(n * TILE, (n + 1) * TILE)

        @pl.when(pos[PAR] == 0)
        def _():
            keep[rows, :] = ref[:, :HD]
            send[rows, :] = ref[:, HD:]

        @pl.when(pos[PAR] != 0)
        def _():
            keep[rows, :] = ref[:, HD:]
            send[rows, :] = ref[:, :HD]


def back_project(pos, w, c0, c1, c2, c3, cot, keep, send):
    for d, ref in enumerate((c0, c1, c2, c3)):
        start = pl.multiple_of(lax.rem(pos[Y] - d + 4, 4) * 32, 32)
        cot[pl.ds(start, 32), :] = ref[...]
    full = cot[...]
    mine = pl.multiple_of(pos[PAR] * HD, HD)
    other = pl.multiple_of((1 - pos[PAR]) * HD, HD)
    keep[...] = dot(w[pl.ds(mine, HD), :], full, NT).astype(BF16)
    send[...] = dot(w[pl.ds(other, HD), :], full, NT).astype(BF16)


def bias_rows(pos, mask, query_x):
    lane = lax.broadcasted_iota(jnp.int32, (1, BLK), 1)
    par = pos[PAR]
    query = (query_x * 4 + pos[ZH]) * 2
    rows = []
    for e in range(4):
        key = (pos[X] * 4 + lax.rem(pos[ZH] - e + 4, 4)) * 2
        for tile in (par, 1 - par):
            near = jnp.where(mask[query + par, key + tile] > 0, 0.0, LOW)
            far = jnp.where(mask[query + 1 - par, key + tile] > 0, 0.0, LOW)
            rows.append(jnp.where(lane < TILE, near, far))
    return rows


def scores_of(keys, queries, rows, e):
    raw = dot(keys, queries, NT) * (SCALE * LOG2E)
    return jnp.concatenate([raw[:TILE] + rows[2 * e], raw[TILE:] + rows[2 * e + 1]], axis=0)


def split3(value):
    high = value.astype(BF16).astype(F32)
    rest = value - high
    middle = rest.astype(BF16).astype(F32)
    low = (rest - middle).astype(BF16).astype(F32)
    return high, middle, low


def forward(pos, mask, kv0, kv1, kv2, kv3, qd0, qd1, qd2, qd3, p0, p1, p2, p3, qd, part, stats):
    kvs = (kv0, kv1, kv2, kv3)
    for d, ref in enumerate((qd0, qd1, qd2, qd3)):
        qd[d] = ref[...]
    values_t = [kv[BLK:, :].astype(F32).T.astype(BF16) for kv in kvs]

    def block(d, carry):
        query_x = lax.rem(pos[X] - d + 4, 4)
        rows = bias_rows(pos, mask, query_x)
        queries = qd[d, :BLK, :]
        scores = [scores_of(kvs[e][:BLK, :], queries, rows, e) for e in range(4)]
        largest = functools.reduce(
            jnp.maximum, [jnp.max(s, axis=0, keepdims=True) for s in scores]
        )
        largest = jnp.maximum(largest, 0.1 * LOW)
        total = jnp.zeros((1, BLK), F32)
        summed = jnp.zeros((HD, BLK), F32)
        for e in range(4):
            weights = jnp.exp2(scores[e] - largest)
            total = total + jnp.sum(weights, axis=0, keepdims=True)
            summed = summed + dot(values_t[e], weights.astype(BF16))
        some = total > 0.0
        safe = jnp.where(some, total, 1.0)
        summed = summed / safe
        lse = jnp.where(some, largest + jnp.log2(safe), LOW)
        grad_t = jnp.concatenate(
            [qd[d, BLK : BLK + TILE, :], qd[d, BLK + TILE :, :]], axis=1
        ).astype(F32)
        delta = jnp.sum(grad_t * summed, axis=0, keepdims=True)
        part[d] = summed.astype(BF16)
        row = lax.broadcasted_iota(jnp.int32, (16, BLK), 0)
        packed = jnp.zeros((16, BLK), F32)
        for n, value in enumerate(split3(lse) + split3(delta)):
            packed = jnp.where(row == n, value, packed)
        stats[pl.ds(pl.multiple_of(query_x * 16, 16), 16), :] = packed.astype(BF16)
        return carry

    lax.fori_loop(0, 4, block, 0)
    for d, ref in enumerate((p0, p1, p2, p3)):
        ref[:HD, :] = part[d]
        ref[HD:, :] = stats[...]


def merge_stats(packs, block):
    lses, deltas = [], []
    for pack in packs:
        s = pack[pl.ds(pl.multiple_of(HD + block * 16, 16), 16), :].astype(F32)
        lses.append(s[0:1] + s[1:2] + s[2:3])
        deltas.append(s[3:4] + s[4:5] + s[5:6])
    largest = functools.reduce(jnp.maximum, lses)
    weights = [jnp.exp2(v - largest) for v in lses]
    total = sum(weights)
    shares = [w / total for w in weights]
    delta = sum(w * v for w, v in zip(shares, deltas))
    return largest + jnp.log2(total), delta, shares


def backward(
    pos, mask, kv0, kv1, kv2, kv3, qd0, qd1, qd2, qd3, p0, p1, p2, p3,
    dkv0, dkv1, dkv2, dkv3, dq0, dq1, dq2, dq3, qd, dq, dkv,
):
    kvs = (kv0, kv1, kv2, kv3)
    for d, ref in enumerate((qd0, qd1, qd2, qd3)):
        qd[d] = ref[...]
    dkv[...] = jnp.zeros_like(dkv)
    keys_t = [kv[:BLK, :].astype(F32).T.astype(BF16) for kv in kvs]

    def block(d, carry):
        query_x = lax.rem(pos[X] - d + 4, 4)
        rows = bias_rows(pos, mask, query_x)
        lse, delta, _ = merge_stats((p0, p1, p2, p3), query_x)
        queries = qd[d, :BLK, :]
        grad_t = jnp.concatenate([qd[d, BLK : BLK + TILE, :], qd[d, BLK + TILE :, :]], axis=1)
        grad_query = jnp.zeros((HD, BLK), F32)
        for e in range(4):
            probs = jnp.exp2(scores_of(kvs[e][:BLK, :], queries, rows, e) - lse)
            grad_probs = dot(kvs[e][BLK:, :], grad_t)
            grad_scores = (probs * (grad_probs - delta)).astype(BF16)
            dkv[e, BLK:, :] += dot(probs.astype(BF16), grad_t, NT)
            dkv[e, :BLK, :] += dot(grad_scores, queries)
            grad_query = grad_query + dot(keys_t[e], grad_scores)
        dq[d] = (grad_query * SCALE).astype(BF16)
        return carry

    lax.fori_loop(0, 4, block, 0)
    for e, ref in enumerate((dkv0, dkv1, dkv2, dkv3)):
        ref[:BLK, :] = (dkv[e, :BLK, :] * SCALE).astype(BF16)
        ref[BLK:, :] = dkv[e, BLK:, :].astype(BF16)
    for d, ref in enumerate((dq0, dq1, dq2, dq3)):
        ref[...] = dq[d]


def attend(pos, p0, p1, p2, p3, att, send):
    packs = (p0, p1, p2, p3)
    _, _, shares = merge_stats(packs, pos[X])
    out = sum(w * p[:HD, :].astype(F32) for w, p in zip(shares, packs)).astype(BF16)
    att[...] = out
    send[...] = out[:, TILE:]


def weight_part(pos, att, near, far, keep, send):
    both = dot(att[:, :TILE], near[...]) + dot(att[:, TILE:], far[...])

    @pl.when(pos[4] == 0)
    def _():
        keep[...] = both[:, :1024]
        send[...] = both[:, 1024:]

    @pl.when(pos[4] != 0)
    def _():
        keep[...] = both[:, 1024:]
        send[...] = both[:, :1024]


def weight_cut(pos, mine, other, b0, b1, b2, b3):
    for d, ref in enumerate((b0, b1, b2, b3)):
        columns = pl.ds(pl.multiple_of(lax.rem(pos[X] + d, 4) * 256, 256), 256)
        ref[...] = (mine[:, columns] + other[:, columns]).astype(BF16)


def sum_four(a, b, c, d, out):
    out[...] = (
        (a[...].astype(F32) + b[...].astype(F32)) + (c[...].astype(F32) + d[...].astype(F32))
    ).astype(out.dtype)


def weight_row(pos, f0, f1, f2, f3, out):
    for d, ref in enumerate((f0, f1, f2, f3)):
        columns = pl.ds(pl.multiple_of(lax.rem(pos[X] - d + 4, 4) * 256, 256), 256)
        out[:, columns] = ref[...]


def weight_out(pos, here, pair, core, both, out):
    par, dp = pos[PAR], pos[4]
    for rows, columns, ref in (
        (par, dp, here), (1 - par, dp, pair), (par, 1 - dp, core), (1 - par, 1 - dp, both),
    ):
        out[
            pl.ds(pl.multiple_of(rows * HD, HD), HD),
            pl.ds(pl.multiple_of(columns * 1024, 1024), 1024),
        ] = ref[...].astype(F32)


def mix(pos, att, other, w, m0, m1, m2, m3, full):
    mine_rows = pl.ds(pl.multiple_of(pos[PAR] * HD, HD), HD)
    other_rows = pl.ds(pl.multiple_of((1 - pos[PAR]) * HD, HD), HD)
    mine_t = att[:, :TILE].astype(F32).T.astype(BF16)
    other_t = other[...].astype(F32).T.astype(BF16)
    full[...] = (dot(mine_t, w[mine_rows, :]) + dot(other_t, w[other_rows, :])).astype(BF16)
    for d, ref in enumerate((m0, m1, m2, m3)):
        ref[...] = full[pl.ds(pl.multiple_of(lax.rem(pos[Y] + d, 4) * 32, 32), 32), :]


def gather_grads(k0, k1, k2, k3, q0, q1, q2, q3, keep, send):
    kv = (k0[...].astype(F32) + k1[...].astype(F32)) + (k2[...].astype(F32) + k3[...].astype(F32))
    q = (q0[...].astype(F32) + q1[...].astype(F32)) + (q2[...].astype(F32) + q3[...].astype(F32))
    keep[:TILE, :] = q[:, :TILE].T.astype(BF16)
    send[:TILE, :] = q[:, TILE:].T.astype(BF16)
    keep[TILE : 2 * TILE, :] = kv[:TILE].astype(BF16)
    send[TILE : 2 * TILE, :] = kv[TILE:BLK].astype(BF16)
    keep[2 * TILE :, :] = kv[BLK : BLK + TILE].astype(BF16)
    send[2 * TILE :, :] = kv[BLK + TILE :].astype(BF16)


def join_heads(pos, mine, other, q, k, v):
    for n, ref in enumerate((q, k, v)):
        rows = slice(n * TILE, (n + 1) * TILE)

        @pl.when(pos[PAR] == 0)
        def _():
            ref[:, :HD] = mine[rows, :]
            ref[:, HD:] = other[rows, :]

        @pl.when(pos[PAR] != 0)
        def _():
            ref[:, HD:] = mine[rows, :]
            ref[:, :HD] = other[rows, :]


def over_x(a, d):
    return lax.ppermute(a, "tm", [(i, (i + 8 * d) % 32) for i in range(32)])


def over_z(a, d):
    return lax.ppermute(a, "tm", [(i, i // 8 * 8 + (i + 2 * d) % 8) for i in range(32)])


def over_pair(a):
    return lax.ppermute(a, "tm", [(i, i ^ 1) for i in range(32)])


def over_y(a, d):
    return lax.ppermute(a, "tensor", [(i, (i + d) % 4) for i in range(4)])


def over_core(a):
    return lax.ppermute(a, "dp", [(0, 1), (1, 0)])


def on_device(query_rows, key_rows, value_rows, out_weight, cotangent, tile_mask):
    tm = lax.axis_index("tm")
    pos = jnp.stack(
        [tm // 8, tm % 8 // 2, tm % 2, lax.axis_index("tensor"), lax.axis_index("dp")]
    ).astype(jnp.int32)
    kv_mm = 2 * 1024 * 1024 * HD

    keep, send = call(
        split_heads,
        [((3 * TILE, HD), BF16)] * 2,
        (pos, query_rows[0], key_rows[0], value_rows[0]),
    )
    recv = over_pair(send)
    cots = [cotangent[0]] + [over_y(cotangent[0], d) for d in (1, 3, 2)]
    cots = [cots[0], cots[1], cots[3], cots[2]]
    cot, grad_keep, grad_send = call(
        back_project,
        [((TILE, 2048), BF16), ((HD, TILE), BF16), ((HD, TILE), BF16)],
        (pos, out_weight, *cots),
        flops=2 * TILE * 256 * 2048,
    )
    kv = jnp.concatenate(
        [keep[TILE : 2 * TILE], recv[TILE : 2 * TILE], keep[2 * TILE :], recv[2 * TILE :]]
    )
    kvs = [kv] + [over_z(kv, d) for d in (1, 2, 3)]
    grad_recv = over_pair(grad_send)
    qd = jnp.concatenate([keep[:TILE], recv[:TILE], grad_keep, grad_recv])
    qds = [qd] + [over_x(qd, d) for d in (1, 2, 3)]
    cot_far = over_pair(cot)

    packs = call(
        forward,
        [((192, BLK), BF16)] * 4,
        (pos, tile_mask, *kvs, *qds),
        flops=2 * kv_mm,
        scratch=[
            pltpu.VMEM((4, 2 * BLK, HD), BF16),
            pltpu.VMEM((4, HD, BLK), BF16),
            pltpu.VMEM((64, BLK), BF16),
        ],
        smem=2,
    )
    packs = [packs[0]] + [over_x(packs[d], -d) for d in (1, 2, 3)]

    att, att_send = call(attend, [((HD, BLK), BF16), ((HD, TILE), BF16)], (pos, *packs))
    gw_keep, gw_send = call(
        weight_part,
        [((HD, 1024), F32)] * 2,
        (pos, att, cot, cot_far),
        flops=2 * HD * BLK * 2048,
    )
    gw_recv = over_core(gw_send)
    cuts = call(weight_cut, [((HD, 256), BF16)] * 4, (pos, gw_keep, gw_recv))
    cuts = [cuts[0]] + [over_x(cuts[d], d) for d in (1, 2, 3)]
    (share,) = call(sum_four, [((HD, 256), BF16)], cuts, smem=0)
    shares = [share] + [over_z(share, d) for d in (1, 2, 3)]
    (done,) = call(sum_four, [((HD, 256), BF16)], shares, smem=0)
    dones = [done] + [over_x(done, d) for d in (1, 2, 3)]
    (here,) = call(weight_row, [((HD, 1024), BF16)], (pos, *dones))
    pair = over_pair(here)
    core, both = over_core(here), over_core(pair)
    (grad_weight,) = call(weight_out, [((256, 2048), F32)], (pos, here, pair, core, both))

    att_recv = over_pair(att_send)
    mixes = call(
        mix,
        [((32, 2048), BF16)] * 4,
        (pos, att, att_recv, out_weight),
        flops=2 * TILE * 256 * 2048,
        scratch=[pltpu.VMEM((TILE, 2048), BF16)],
    )
    mixes = [mixes[0]] + [over_y(mixes[d], d) for d in (1, 2, 3)]
    (mixed,) = call(sum_four, [((32, 2048), BF16)], mixes, smem=0)

    grads = call(
        backward,
        [((2 * BLK, HD), BF16)] * 4 + [((HD, BLK), BF16)] * 4,
        (pos, tile_mask, *kvs, *qds, *packs),
        flops=5 * kv_mm,
        scratch=[
            pltpu.VMEM((4, 2 * BLK, HD), BF16),
            pltpu.VMEM((4, HD, BLK), BF16),
            pltpu.VMEM((4, 2 * BLK, HD), F32),
        ],
        smem=2,
    )
    dkvs = [grads[0]] + [over_z(grads[d], -d) for d in (1, 2, 3)]
    dqs = [grads[4]] + [over_x(grads[4 + d], -d) for d in (1, 2, 3)]
    out_keep, out_send = call(
        gather_grads, [((3 * TILE, HD), BF16)] * 2, (*dkvs, *dqs), smem=0
    )
    out_recv = over_pair(out_send)
    grad_q, grad_k, grad_v = call(
        join_heads, [((TILE, 2 * HD), BF16)] * 3, (pos, out_keep, out_recv)
    )
    return (mixed[None], grad_q[None], grad_k[None], grad_v[None], grad_weight)


def solution(mesh):
    rows = P("dp", "tm", "tensor")
    blocks = P("dp", ("tm", "tensor"), None)
    weight = P("tensor", None)
    return jax.shard_map(
        on_device,
        mesh=mesh,
        in_specs=(rows, rows, rows, weight, blocks, P()),
        out_specs=(blocks, rows, rows, rows, weight),
        check_vma=False,
    )
```

```python
import functools
import math

import jax
import jax.numpy as jnp
from jax import lax
from jax.experimental import pallas as pl
from jax.experimental.pallas import tpu as pltpu
from jax.sharding import Mesh
from jax.sharding import PartitionSpec as P

HD = 128
TILE = 128
BLK = 256
SCALE = HD ** (-0.5)
LOG2E = math.log2(math.e)
LOW = -1e30
F32 = jnp.float32
BF16 = jnp.bfloat16
AXES = ("x", "zh", "par", "y", "core")
X, ZH, PAR, Y, CORE = range(5)
ORDER = (0, 1, 3, 2)
NN = (((1,), (0,)), ((), ()))
NT = (((1,), (1,)), ((), ()))


def dot(a, b, dims=NN):
    return lax.dot_general(a, b, dims, preferred_element_type=F32)


def call(
    body, outs, ins, flops=0, scratch=(), smem=1, vmem=48, after=(), space=pltpu.VMEM,
    out_space=pltpu.VMEM,
):
    specs = [pl.BlockSpec(memory_space=pltpu.SMEM)] * smem
    specs += [pl.BlockSpec(memory_space=space)] * (len(ins) - smem)
    used = len(ins)
    if after:
        specs += [pl.BlockSpec(memory_space=pl.ANY)] * len(after)
        inner = body

        def body(*refs):
            inner(*refs[:used], *refs[used + len(after) :])

    shapes = [jax.ShapeDtypeStruct(s, d) for s, d in outs]
    moved = sum(math.prod(a.shape) * a.dtype.itemsize for a in list(ins) + shapes)
    ins = tuple(ins) + tuple(after)
    return pl.pallas_call(
        body,
        out_shape=shapes,
        in_specs=specs,
        out_specs=[pl.BlockSpec(memory_space=out_space)] * len(outs),
        scratch_shapes=list(scratch),
        compiler_params=pltpu.CompilerParams(vmem_limit_bytes=vmem * 2**20),
        cost_estimate=pl.CostEstimate(flops=flops, bytes_accessed=moved, transcendentals=0),
    )(*ins)


def split_heads(pos, q, k, v, keep, send, sems):
    mine = pl.ds(pl.multiple_of(pos[PAR] * HD, HD), HD)
    other = pl.ds(pl.multiple_of((1 - pos[PAR]) * HD, HD), HD)
    copies = []
    for n, ref in enumerate((q, k, v)):
        rows = pl.ds(n * TILE, TILE)
        for m, (columns, out) in enumerate(((other, send), (mine, keep))):
            copies.append(
                pltpu.make_async_copy(ref.at[:, columns], out.at[rows, :], sems.at[n, m])
            )
            copies[-1].start()
    for copy in copies:
        copy.wait()


def own_blocks(keep, recv, k, v, q):
    for n, ref in ((0, q), (1, k), (2, v)):
        rows = slice(n * TILE, (n + 1) * TILE)
        ref[:TILE, :] = keep[rows, :]
        ref[TILE:, :] = recv[rows, :]


def stack_two(a, b, out):
    rows = a.shape[0]
    out[:rows, :] = a[...]
    out[rows:, :] = b[...]


def stack_pairs(k0, k1, v0, v1, q0, q1, k, v, q):
    stack_two(k0, k1, k)
    stack_two(v0, v1, v)
    stack_two(q0, q1, q)


def join_rows(pos, pair, other, near, far):
    for n in range(4):
        ref = (pair, other)[n // 2]
        start = (n % 2) * 64
        rows = pl.ds(pl.multiple_of((pos[Y] ^ ORDER[n]) * 32, 32), 32)
        near[rows, :] = ref[start : start + 32, :]
        far[rows, :] = ref[start + 32 : start + 64, :]


def bias_rows(pos, mask, query_x):
    lane = lax.broadcasted_iota(jnp.int32, (1, BLK), 1)
    par = pos[PAR]
    query = (query_x * 4 + pos[ZH]) * 2
    rows = []
    for e in range(4):
        key = (pos[X] * 4 + (pos[ZH] ^ e)) * 2
        for tile in (par, 1 - par):
            near = jnp.where(mask[query + par, key + tile] > 0, 0.0, LOW)
            far = jnp.where(mask[query + 1 - par, key + tile] > 0, 0.0, LOW)
            rows.append(jnp.where(lane < TILE, near, far))
    return rows


def scores_of(keys, queries, rows, e):
    raw = dot(keys, queries, NT) * (SCALE * LOG2E)
    return jnp.concatenate([raw[:TILE] + rows[2 * e], raw[TILE:] + rows[2 * e + 1]], axis=0)


def split3(value):
    high = value.astype(BF16).astype(F32)
    rest = value - high
    middle = rest.astype(BF16).astype(F32)
    low = (rest - middle).astype(BF16).astype(F32)
    return high, middle, low


def pack_rows(values):
    row = lax.broadcasted_iota(jnp.int32, (16, BLK), 0)
    packed = jnp.zeros((16, BLK), F32)
    for n, value in enumerate(values):
        packed = jnp.where(row == n, value, packed)
    return packed.astype(BF16)


def halves(ref):
    rows = ref.shape[0] // 2
    return ref[:rows, :], ref[rows:, :]


def by_place(kp, kf, vp, vn):
    (k0, k1), (k3, k2) = halves(kp), halves(kf)
    (v0, v3), (v1, v2) = halves(vp), halves(vn)
    return (k0, k1, k2, k3), (v0, v1, v2, v3)


def forward(pos, mask, kp, kf, vp, vn, qp, qf, p0, p1, p2, p3, q, part):
    keys, values = by_place(kp, kf, vp, vn)
    values_t = [v.astype(F32).T.astype(BF16) for v in values]
    for n in range(4):
        start = (n % 2) * BLK
        q[pos[X] ^ ORDER[n]] = (qp, qf)[n // 2][start : start + BLK, :]

    def block(x, carry):
        rows = bias_rows(pos, mask, x)
        scores = [scores_of(keys[e], q[x], rows, e) for e in range(4)]
        largest = functools.reduce(
            jnp.maximum, [jnp.max(s, axis=0, keepdims=True) for s in scores]
        )
        largest = jnp.maximum(largest, 0.1 * LOW)
        total = jnp.zeros((1, BLK), F32)
        summed = jnp.zeros((HD, BLK), F32)
        for e in range(4):
            weights = jnp.exp2(scores[e] - largest)
            total = total + jnp.sum(weights, axis=0, keepdims=True)
            summed = summed + dot(values_t[e], weights.astype(BF16))
        some = total > 0.0
        safe = jnp.where(some, total, 1.0)
        part[x, :HD, :] = (summed / safe).astype(BF16)
        part[x, HD:, :] = pack_rows(split3(jnp.where(some, largest + jnp.log2(safe), LOW)))
        return carry

    lax.fori_loop(0, 4, block, 0)
    for n, ref in enumerate((p0, p1, p2, p3)):
        ref[...] = part[pos[X] ^ ORDER[n]]


def backward(
    pos, mask, kp, kf, vp, vn, qp, qf, s0, s1, s2, s3,
    dk, dk_far, dv, dv_near, dq, dq_far, q, g, stats, part, acc,
):
    keys, values = by_place(kp, kf, vp, vn)
    keys_t = [k.astype(F32).T.astype(BF16) for k in keys]
    for n, stat in enumerate((s0, s1, s2, s3)):
        x = pos[X] ^ ORDER[n]
        q[x] = (qp, qf)[n // 2][(n % 2) * BLK : (n % 2 + 1) * BLK, :]
        g[x] = stat[HD : 2 * HD, :]
        stats[x] = stat[2 * HD :, :]
    acc[...] = jnp.zeros_like(acc)

    def block(x, carry):
        rows = bias_rows(pos, mask, x)
        queries, grad_t = q[x], g[x]
        s = stats[x].astype(F32)
        lse = s[0:1] + s[1:2] + s[2:3]
        delta = s[3:4] + s[4:5] + s[5:6]
        grad_query = jnp.zeros((HD, BLK), F32)
        for e in range(4):
            probs = jnp.exp2(scores_of(keys[e], queries, rows, e) - lse)
            grad_probs = dot(values[e], grad_t)
            grad_scores = (probs * (grad_probs - delta)).astype(BF16)
            acc[e, BLK:, :] += dot(probs.astype(BF16), grad_t, NT)
            acc[e, :BLK, :] += dot(grad_scores, queries)
            grad_query = grad_query + dot(keys_t[e], grad_scores)
        part[x] = (grad_query * SCALE).astype(BF16)
        return carry

    lax.fori_loop(0, 4, block, 0)
    for n, (e, k, f, v) in enumerate(
        ((0, dk, 0, dv), (1, dk, 3, dv), (3, dk_far, 1, dv_near), (2, dk_far, 2, dv_near))
    ):
        rows = slice((n % 2) * BLK, (n % 2 + 1) * BLK)
        k[rows, :] = (acc[e, :BLK, :] * SCALE).astype(BF16)
        v[rows, :] = acc[f, BLK:, :].astype(BF16)
    for n in range(4):
        ref = (dq, dq_far)[n // 2]
        ref[(n % 2) * HD : (n % 2 + 1) * HD, :] = part[pos[X] ^ ORDER[n]]


def back_project(pos, w, near, far, grads):
    head = w[pl.ds(pl.multiple_of(pos[PAR] * HD, HD), HD), :]
    grads[:, :TILE] = dot(head, near[...], NT).astype(BF16)
    grads[:, TILE:] = dot(head, far[...], NT).astype(BF16)


def attend(pos, p0, p1, p2, p3, grads, near, far, att, stats, keep, send):
    lses, parts = [], []
    for pack in (p0, p1, p2, p3):
        parts.append(pack[:HD, :].astype(F32))
        s = pack[HD:, :].astype(F32)
        lses.append(s[0:1] + s[1:2] + s[2:3])
    largest = functools.reduce(jnp.maximum, lses)
    weights = [jnp.exp2(v - largest) for v in lses]
    total = sum(weights)
    out = sum((w / total) * p for w, p in zip(weights, parts)).astype(BF16)
    att[...] = out
    delta = jnp.sum(grads[...].astype(F32) * out.astype(F32), axis=0, keepdims=True)
    stats[...] = pack_rows(split3(largest + jnp.log2(total)) + split3(delta))
    both = dot(out[:, :TILE], near[...]) + dot(out[:, TILE:], far[...])

    @pl.when(pos[CORE] == 0)
    def _():
        keep[...] = both[:, :1024]
        send[...] = both[:, 1024:]

    @pl.when(pos[CORE] != 0)
    def _():
        keep[...] = both[:, 1024:]
        send[...] = both[:, :1024]


def weight_cut(pos, mine, other, grads, stats, b0, b1, b2, b3):
    for n, ref in enumerate((b0, b1, b2, b3)):
        columns = pl.ds(pl.multiple_of((pos[X] ^ ORDER[n]) * BLK, BLK), BLK)
        ref[:HD, :] = (mine[:, columns] + other[:, columns]).astype(BF16)
        ref[HD : 2 * HD, :] = grads[...]
        ref[2 * HD :, :] = stats[...]


def add(a, b):
    return a.astype(F32) + b.astype(F32)


def sum_cuts(a, b, c, d, out):
    out[...] = (add(a[:HD, :], b[:HD, :]) + add(c[:HD, :], d[:HD, :])).astype(BF16)


def sum_two(a, b, out):
    out[...] = add(a[...], b[...]).astype(BF16)


def sum_split(a, b, keep, send):
    total = add(a[...], b[...]).astype(BF16)
    rows = keep.shape[0]
    keep[...] = total[:rows]
    send[...] = total[rows:]


def weight_stack(pos, mine, other, out):
    out[pl.ds(pl.multiple_of(pos[PAR] * HD, HD), HD), :] = mine[...]
    out[pl.ds(pl.multiple_of((1 - pos[PAR]) * HD, HD), HD), :] = other[...]


def weight_row(pos, f0, f1, f2, f3, out):
    for n, ref in enumerate((f0, f1, f2, f3)):
        columns = pl.ds(pl.multiple_of((pos[X] ^ ORDER[n]) * BLK, BLK), BLK)
        out[:, columns] = ref[...]


def mix(pos, att, other, w, out, out_far, full):
    mine_rows = pl.ds(pl.multiple_of(pos[PAR] * HD, HD), HD)
    other_rows = pl.ds(pl.multiple_of((1 - pos[PAR]) * HD, HD), HD)
    mine_t = att[:, :TILE].astype(F32).T.astype(BF16)
    other_t = other[...].astype(F32).T.astype(BF16)
    full[...] = (dot(mine_t, w[mine_rows, :]) + dot(other_t, w[other_rows, :])).astype(BF16)
    for n in range(4):
        rows = pl.ds(pl.multiple_of((pos[Y] ^ ORDER[n]) * 32, 32), 32)
        (out, out_far)[n // 2][(n % 2) * 32 : (n % 2 + 1) * 32, :] = full[rows, :]


def gather_grads(k, k_near, v, v_far, q, q_near, keep, send):
    q = add(q[...], q_near[...])
    keep[:TILE, :] = q[:, :TILE].T.astype(BF16)
    send[:TILE, :] = q[:, TILE:].T.astype(BF16)
    for n, (mine, other) in enumerate(((k, k_near), (v, v_far))):
        total = add(mine[...], other[...]).astype(BF16)
        rows = slice((n + 1) * TILE, (n + 2) * TILE)
        keep[rows, :] = total[:TILE]
        send[rows, :] = total[TILE:]


def finish(pos, mine, other, here, core, q, k, v, weight):
    for half, ref in ((pos[CORE], here), (1 - pos[CORE], core)):
        columns = pl.ds(pl.multiple_of(half * 1024, 1024), 1024)
        weight[:, columns] = ref[...].astype(F32)
    for n, ref in enumerate((q, k, v)):
        rows = slice(n * TILE, (n + 1) * TILE)

        @pl.when(pos[PAR] == 0)
        def _():
            ref[:, :HD] = mine[rows, :]
            ref[:, HD:] = other[rows, :]

        @pl.when(pos[PAR] != 0)
        def _():
            ref[:, HD:] = mine[rows, :]
            ref[:, :HD] = other[rows, :]


def near(a, axis):
    return lax.ppermute(a, axis, [(0, 1), (1, 0), (2, 3), (3, 2)])


def far(a, axis):
    return lax.ppermute(a, axis, [(0, 3), (3, 0), (1, 2), (2, 1)])


def opposite(a, axis):
    return lax.ppermute(a, axis, [(0, 2), (2, 0), (1, 3), (3, 1)])


def over_pair(a):
    return lax.ppermute(a, "par", [(0, 1), (1, 0)])


def over_core(a):
    return lax.ppermute(a, "core", [(0, 1), (1, 0)])


def on_device(query_rows, key_rows, value_rows, out_weight, cotangent, tile_mask):
    pos = jnp.stack([lax.axis_index(name) for name in AXES]).astype(jnp.int32)
    kv_mm = 2 * 1024 * 1024 * HD

    keep, send = call(
        split_heads,
        [((3 * TILE, HD), BF16)] * 2,
        (pos, query_rows[0], key_rows[0], value_rows[0]),
        scratch=[pltpu.SemaphoreType.DMA((3, 2))],
        space=pltpu.HBM,
        out_space=pltpu.HBM,
    )
    recv = over_pair(send)
    rows_far = over_pair(cotangent[0])
    k, v, q = call(own_blocks, [((BLK, HD), BF16)] * 3, (keep, recv), smem=0)
    (rows,) = call(stack_two, [((64, 2048), BF16)], (cotangent[0], rows_far), smem=0, after=(recv,))
    kp, vp, qp = call(
        stack_pairs,
        [((2 * BLK, HD), BF16)] * 3,
        (k, near(k, "zh"), v, far(v, "zh"), q, near(q, "x")),
        smem=0,
    )
    (rows,) = call(stack_two, [((TILE, 2048), BF16)], (rows, near(rows, "y")), smem=0, after=(kp,))
    kf, vn, qf, rows_far = far(kp, "zh"), near(vp, "zh"), far(qp, "x"), far(rows, "y")

    packs = call(
        forward,
        [((HD + 16, BLK), BF16)] * 4,
        (pos, tile_mask, kp, kf, vp, vn, qp, qf),
        flops=2 * kv_mm,
        scratch=[pltpu.VMEM((4, BLK, HD), BF16), pltpu.VMEM((4, HD + 16, BLK), BF16)],
        smem=2,
    )
    packs = [packs[0], near(packs[1], "x"), far(packs[2], "x"), opposite(packs[3], "x")]

    cot, cot_far = call(join_rows, [((TILE, 2048), BF16)] * 2, (pos, rows, rows_far))
    (grads,) = call(
        back_project,
        [((HD, BLK), BF16)],
        (pos, out_weight, cot, cot_far),
        flops=2 * HD * BLK * 2048,
    )
    att, stats, gw_keep, gw_send = call(
        attend,
        [((HD, BLK), BF16), ((16, BLK), BF16)] + [((HD, 1024), F32)] * 2,
        (pos, *packs, grads, cot, cot_far),
        flops=2 * HD * BLK * 2048,
    )
    gw_recv = over_core(gw_send)
    cuts = call(
        weight_cut, [((2 * HD + 16, BLK), BF16)] * 4, (pos, gw_keep, gw_recv, grads, stats)
    )
    cuts = [cuts[0], near(cuts[1], "x"), far(cuts[2], "x"), opposite(cuts[3], "x")]
    (share,) = call(sum_cuts, [((HD, BLK), BF16)], cuts, smem=0)

    dk, dk_far, dv, dv_near, dq, dq_far = call(
        backward,
        [((2 * BLK, HD), BF16)] * 4 + [((2 * HD, BLK), BF16)] * 2,
        (pos, tile_mask, kp, kf, vp, vn, qp, qf, *cuts),
        flops=5 * kv_mm,
        scratch=[
            pltpu.VMEM((4, BLK, HD), BF16),
            pltpu.VMEM((4, HD, BLK), BF16),
            pltpu.VMEM((4, 16, BLK), BF16),
            pltpu.VMEM((4, HD, BLK), BF16),
            pltpu.VMEM((4, 2 * BLK, HD), F32),
        ],
        smem=2,
        after=(share,),
    )
    (near_sum,) = call(
        sum_two, [((HD, BLK), BF16)], (share, near(share, "zh")), smem=0, after=(dq,)
    )
    (done,) = call(sum_two, [((HD, BLK), BF16)], (near_sum, far(near_sum, "zh")), smem=0)
    dq_far = lax.optimization_barrier((dq_far, near_sum))[0]
    dk_far, dv_near, _ = lax.optimization_barrier((dk_far, dv_near, done))

    att_far = over_pair(att[:, TILE:])
    mixed, mixed_far = call(
        mix,
        [((64, 2048), BF16)] * 2,
        (pos, att, att_far, out_weight),
        flops=2 * TILE * 256 * 2048,
        scratch=[pltpu.VMEM((TILE, 2048), BF16)],
    )
    mixed, mixed_near = call(
        sum_split, [((32, 2048), BF16)] * 2, (mixed, far(mixed_far, "y")), smem=0
    )
    (mixed,) = call(sum_two, [((32, 2048), BF16)], (mixed, near(mixed_near, "y")), smem=0)

    dk, dk_near = call(
        sum_split, [((BLK, HD), BF16)] * 2, (dk, far(dk_far, "zh")), smem=0
    )
    dv, dv_far = call(
        sum_split, [((BLK, HD), BF16)] * 2, (dv, near(dv_near, "zh")), smem=0
    )
    dq, dq_near = call(sum_split, [((HD, BLK), BF16)] * 2, (dq, far(dq_far, "x")), smem=0)
    dq_near = lax.optimization_barrier((dq_near, dk_near))[0]
    out_keep, out_send = call(
        gather_grads,
        [((3 * TILE, HD), BF16)] * 2,
        (dk, near(dk_near, "zh"), dv, far(dv_far, "zh"), dq, near(dq_near, "x")),
        smem=0,
    )

    (stack,) = call(weight_stack, [((2 * HD, BLK), BF16)], (pos, done, over_pair(done)), after=(mixed,))
    stacks = [stack, near(stack, "x"), far(stack, "x"), opposite(stack, "x")]
    (here,) = call(
        weight_row, [((2 * HD, 1024), BF16)], (pos, *stacks), after=(out_send,)
    )
    grad_q, grad_k, grad_v, grad_weight = call(
        finish,
        [((TILE, 2 * HD), BF16)] * 3 + [((2 * HD, 2048), F32)],
        (pos, out_keep, over_pair(out_send), here, over_core(here)),
    )
    return (mixed[None], grad_q[None], grad_k[None], grad_v[None], grad_weight)


def solution(mesh):
    mesh = Mesh(mesh.devices.reshape(4, 4, 2, 4, 2), AXES)
    tokens = ("x", "zh", "par")
    rows = P("core", tokens, "y")
    blocks = P("core", (*tokens, "y"), None)
    weight = P("y", None)
    return jax.shard_map(
        on_device,
        mesh=mesh,
        in_specs=(rows, rows, rows, weight, blocks, P()),
        out_specs=(blocks, rows, rows, rows, weight),
        check_vma=False,
    )
```

```python
import functools
import math

import jax
import jax.numpy as jnp
from jax import lax
from jax.experimental import pallas as pl
from jax.experimental.pallas import tpu as pltpu
from jax.sharding import Mesh
from jax.sharding import PartitionSpec as P

HD = 128
TILE = 128
BLK = 256
SCALE = HD ** (-0.5)
LOG2E = math.log2(math.e)
LOW = -1e30
F32 = jnp.float32
BF16 = jnp.bfloat16
AXES = ("x", "zh", "par", "y", "core")
X, ZH, PAR, Y, CORE = range(5)
ORDER = (0, 1, 3, 2)
NN = (((1,), (0,)), ((), ()))
NT = (((1,), (1,)), ((), ()))


def dot(a, b, dims=NN):
    return lax.dot_general(a, b, dims, preferred_element_type=F32)


def call(
    body, outs, ins, flops=0, scratch=(), smem=1, vmem=48, after=(), space=pltpu.VMEM,
    out_space=pltpu.VMEM,
):
    specs = [pl.BlockSpec(memory_space=pltpu.SMEM)] * smem
    specs += [pl.BlockSpec(memory_space=space)] * (len(ins) - smem)
    used = len(ins)
    if after:
        specs += [pl.BlockSpec(memory_space=pl.ANY)] * len(after)
        inner = body

        def body(*refs):
            inner(*refs[:used], *refs[used + len(after) :])

    shapes = [jax.ShapeDtypeStruct(s, d) for s, d in outs]
    moved = sum(math.prod(a.shape) * a.dtype.itemsize for a in list(ins) + shapes)
    ins = tuple(ins) + tuple(after)
    return pl.pallas_call(
        body,
        out_shape=shapes,
        in_specs=specs,
        out_specs=[pl.BlockSpec(memory_space=out_space)] * len(outs),
        scratch_shapes=list(scratch),
        compiler_params=pltpu.CompilerParams(vmem_limit_bytes=vmem * 2**20),
        cost_estimate=pl.CostEstimate(flops=flops, bytes_accessed=moved, transcendentals=0),
    )(*ins)


def own_blocks(keep, recv, k, v, q):
    for n, ref in ((0, q), (1, k), (2, v)):
        rows = slice(n * TILE, (n + 1) * TILE)
        ref[:TILE, :] = keep[rows, :]
        ref[TILE:, :] = recv[rows, :]


def stack_two(a, b, out):
    rows = a.shape[0]
    out[:rows, :] = a[...]
    out[rows:, :] = b[...]


def stack_pairs(k0, k1, v0, v1, q0, q1, k, v, q):
    stack_two(k0, k1, k)
    stack_two(v0, v1, v)
    stack_two(q0, q1, q)


def join_rows(pos, pair, other, near, far):
    for n in range(4):
        ref = (pair, other)[n // 2]
        start = (n % 2) * 64
        rows = pl.ds(pl.multiple_of((pos[Y] ^ ORDER[n]) * 32, 32), 32)
        near[rows, :] = ref[start : start + 32, :]
        far[rows, :] = ref[start + 32 : start + 64, :]


def bias_rows(pos, mask, query_x):
    lane = lax.broadcasted_iota(jnp.int32, (1, BLK), 1)
    par = pos[PAR]
    query = (query_x * 4 + pos[ZH]) * 2
    rows = []
    for e in ORDER:
        key = (pos[X] * 4 + (pos[ZH] ^ e)) * 2
        for tile in (par, 1 - par):
            near = jnp.where(mask[query + par, key + tile] > 0, 0.0, LOW)
            far = jnp.where(mask[query + 1 - par, key + tile] > 0, 0.0, LOW)
            rows.append(jnp.where(lane < TILE, near, far))
    return rows


def scores_of(keys, queries, rows):
    raw = dot(keys, queries, NT) * (SCALE * LOG2E)
    return jnp.concatenate(
        [raw[t * TILE : (t + 1) * TILE] + row for t, row in enumerate(rows)], axis=0
    )


def split3(value):
    high = value.astype(BF16).astype(F32)
    rest = value - high
    middle = rest.astype(BF16).astype(F32)
    low = (rest - middle).astype(BF16).astype(F32)
    return high, middle, low


def pack_rows(values):
    row = lax.broadcasted_iota(jnp.int32, (16, BLK), 0)
    packed = jnp.zeros((16, BLK), F32)
    for n, value in enumerate(values):
        packed = jnp.where(row == n, value, packed)
    return packed.astype(BF16)


def load_kv(kp, kf, vp, vn):
    keys = jnp.concatenate([kp[...], kf[...]], axis=0)
    values = [vp[:BLK, :], vn[:BLK, :], vp[BLK:, :], vn[BLK:, :]]
    return keys, jnp.concatenate(values, axis=0)


def transposed(a):
    return a.astype(F32).T.astype(BF16)


def query_block(qp, qf, n):
    return (qp, qf)[n // 2][(n % 2) * BLK : (n % 2 + 1) * BLK, :]


def forward(pos, mask, kp, kf, vp, vn, qp, qf, p0, p1, p2, p3):
    keys, values = load_kv(kp, kf, vp, vn)
    values_t = transposed(values)
    for n, pack in enumerate((p0, p1, p2, p3)):
        rows = bias_rows(pos, mask, pos[X] ^ ORDER[n])
        queries = query_block(qp, qf, n)
        scores = [
            scores_of(keys[e * BLK : (e + 1) * BLK], queries, rows[2 * e : 2 * e + 2])
            for e in range(4)
        ]
        largest = functools.reduce(
            jnp.maximum, [jnp.max(block, axis=0, keepdims=True) for block in scores]
        )
        largest = jnp.maximum(largest, 0.1 * LOW)
        total = jnp.zeros((1, BLK), F32)
        summed = jnp.zeros((HD, BLK), F32)
        for e in range(4):
            weights = jnp.exp2(scores[e] - largest)
            total = total + jnp.sum(weights, axis=0, keepdims=True)
            summed = summed + dot(values_t[:, e * BLK : (e + 1) * BLK], weights.astype(BF16))
        some = total > 0.0
        safe = jnp.where(some, total, 1.0)
        pack[:HD, :] = (summed / safe).astype(BF16)
        pack[HD:, :] = pack_rows(split3(jnp.where(some, largest + jnp.log2(safe), LOW)))


def backward(
    pos, mask, kp, kf, vp, vn, qp, qf, s0, s1, s2, s3,
    dk, dk_far, dv, dv_near, dq, dq_far, probs_of, scores_grad_of,
):
    keys, values = load_kv(kp, kf, vp, vn)
    keys_t = transposed(keys)
    for n, ref in enumerate((s0, s1, s2, s3)):
        rows = bias_rows(pos, mask, pos[X] ^ ORDER[n])
        s = ref[2 * HD :, :].astype(F32)
        lse = s[0:1] + s[1:2] + s[2:3]
        delta = s[3:4] + s[4:5] + s[5:6]
        probs = jnp.exp2(scores_of(keys, query_block(qp, qf, n), rows) - lse)
        grad_probs = dot(values, ref[HD : 2 * HD, :])
        grad_scores = (probs * (grad_probs - delta)).astype(BF16)
        columns = slice(n * BLK, (n + 1) * BLK)
        probs_of[:, columns] = probs.astype(BF16)
        scores_grad_of[:, columns] = grad_scores
        out = (dq, dq_far)[n // 2]
        out[(n % 2) * HD : (n % 2 + 1) * HD, :] = (dot(keys_t, grad_scores) * SCALE).astype(BF16)
    queries = jnp.concatenate([qp[...], qf[...]], axis=0)
    grads = jnp.concatenate([ref[HD : 2 * HD, :] for ref in (s0, s1, s2, s3)], axis=1)
    for n in range(4):
        block = slice(n * BLK, (n + 1) * BLK)
        half = slice((n % 2) * BLK, (n % 2 + 1) * BLK)
        out = (dk, dk_far)[n // 2]
        out[half, :] = (dot(scores_grad_of[block, :], queries) * SCALE).astype(BF16)
        half = slice((n // 2) * BLK, (n // 2 + 1) * BLK)
        out = (dv, dv_near)[n % 2]
        out[half, :] = dot(probs_of[block, :], grads, NT).astype(BF16)


def back_project(pos, w, near, far, grads):
    head = w[pl.ds(pl.multiple_of(pos[PAR] * HD, HD), HD), :]
    grads[:, :TILE] = dot(head, near[...], NT).astype(BF16)
    grads[:, TILE:] = dot(head, far[...], NT).astype(BF16)


def attend(pos, p0, p1, p2, p3, grads, near, far, att, stats, keep, send):
    lses, parts = [], []
    for pack in (p0, p1, p2, p3):
        parts.append(pack[:HD, :].astype(F32))
        s = pack[HD:, :].astype(F32)
        lses.append(s[0:1] + s[1:2] + s[2:3])
    largest = functools.reduce(jnp.maximum, lses)
    weights = [jnp.exp2(v - largest) for v in lses]
    total = sum(weights)
    out = sum((w / total) * p for w, p in zip(weights, parts)).astype(BF16)
    att[...] = out
    delta = jnp.sum(grads[...].astype(F32) * out.astype(F32), axis=0, keepdims=True)
    stats[...] = pack_rows(split3(largest + jnp.log2(total)) + split3(delta))
    both = dot(out[:, :TILE], near[...]) + dot(out[:, TILE:], far[...])

    @pl.when(pos[CORE] == 0)
    def _():
        keep[...] = both[:, :1024]
        send[...] = both[:, 1024:]

    @pl.when(pos[CORE] != 0)
    def _():
        keep[...] = both[:, 1024:]
        send[...] = both[:, :1024]


def weight_cut(pos, mine, other, grads, stats, b0, b1, b2, b3):
    for n, ref in enumerate((b0, b1, b2, b3)):
        columns = pl.ds(pl.multiple_of((pos[X] ^ ORDER[n]) * BLK, BLK), BLK)
        ref[:HD, :] = (mine[:, columns] + other[:, columns]).astype(BF16)
        ref[HD : 2 * HD, :] = grads[...]
        ref[2 * HD :, :] = stats[...]


def add(a, b):
    return a.astype(F32) + b.astype(F32)


def sum_cuts(a, b, c, d, out):
    out[...] = (add(a[:HD, :], b[:HD, :]) + add(c[:HD, :], d[:HD, :])).astype(BF16)


def sum_two(a, b, out):
    out[...] = add(a[...], b[...]).astype(BF16)


def sum_split(a, b, keep, send):
    total = add(a[...], b[...]).astype(BF16)
    rows = keep.shape[0]
    keep[...] = total[:rows]
    send[...] = total[rows:]


def weight_stack(pos, mine, other, out):
    out[pl.ds(pl.multiple_of(pos[PAR] * HD, HD), HD), :] = mine[...]
    out[pl.ds(pl.multiple_of((1 - pos[PAR]) * HD, HD), HD), :] = other[...]


def weight_row(pos, f0, f1, f2, f3, out):
    for n, ref in enumerate((f0, f1, f2, f3)):
        columns = pl.ds(pl.multiple_of((pos[X] ^ ORDER[n]) * BLK, BLK), BLK)
        out[:, columns] = ref[...]


def mix(pos, att, other, w, out, out_far, full):
    mine_rows = pl.ds(pl.multiple_of(pos[PAR] * HD, HD), HD)
    other_rows = pl.ds(pl.multiple_of((1 - pos[PAR]) * HD, HD), HD)
    mine_t = att[:, :TILE].astype(F32).T.astype(BF16)
    other_t = other[...].astype(F32).T.astype(BF16)
    full[...] = (dot(mine_t, w[mine_rows, :]) + dot(other_t, w[other_rows, :])).astype(BF16)
    for n in range(4):
        rows = pl.ds(pl.multiple_of((pos[Y] ^ ORDER[n]) * 32, 32), 32)
        (out, out_far)[n // 2][(n % 2) * 32 : (n % 2 + 1) * 32, :] = full[rows, :]


def gather_grads(k, k_near, v, v_far, q, q_near, keep, send):
    q = add(q[...], q_near[...])
    keep[:TILE, :] = q[:, :TILE].T.astype(BF16)
    send[:TILE, :] = q[:, TILE:].T.astype(BF16)
    for n, (mine, other) in enumerate(((k, k_near), (v, v_far))):
        total = add(mine[...], other[...]).astype(BF16)
        rows = slice((n + 1) * TILE, (n + 2) * TILE)
        keep[rows, :] = total[:TILE]
        send[rows, :] = total[TILE:]


def finish(pos, mine, other, here, core, q, k, v, weight):
    for half, ref in ((pos[CORE], here), (1 - pos[CORE], core)):
        columns = pl.ds(pl.multiple_of(half * 1024, 1024), 1024)
        weight[:, columns] = ref[...].astype(F32)
    for n, ref in enumerate((q, k, v)):
        rows = slice(n * TILE, (n + 1) * TILE)

        @pl.when(pos[PAR] == 0)
        def _():
            ref[:, :HD] = mine[rows, :]
            ref[:, HD:] = other[rows, :]

        @pl.when(pos[PAR] != 0)
        def _():
            ref[:, HD:] = mine[rows, :]
            ref[:, :HD] = other[rows, :]


def near(a, axis):
    return lax.ppermute(a, axis, [(0, 1), (1, 0), (2, 3), (3, 2)])


def far(a, axis):
    return lax.ppermute(a, axis, [(0, 3), (3, 0), (1, 2), (2, 1)])


def opposite(a, axis):
    return lax.ppermute(a, axis, [(0, 2), (2, 0), (1, 3), (3, 1)])


def over_pair(a):
    return lax.ppermute(a, "par", [(0, 1), (1, 0)])


def over_core(a):
    return lax.ppermute(a, "core", [(0, 1), (1, 0)])


def on_device(query_rows, key_rows, value_rows, out_weight, cotangent, tile_mask):
    pos = jnp.stack([lax.axis_index(name) for name in AXES]).astype(jnp.int32)
    kv_mm = 2 * 1024 * 1024 * HD

    inputs = (query_rows[0], key_rows[0], value_rows[0])
    first = pos[PAR] == 0
    send = jnp.concatenate([jnp.where(first, rows[:, HD:], rows[:, :HD]) for rows in inputs])
    keep = jnp.concatenate([jnp.where(first, rows[:, :HD], rows[:, HD:]) for rows in inputs])
    recv = over_pair(send)
    rows_far = over_pair(cotangent[0])
    k, v, q = call(own_blocks, [((BLK, HD), BF16)] * 3, (keep, recv), smem=0)
    (rows,) = call(stack_two, [((64, 2048), BF16)], (cotangent[0], rows_far), smem=0, after=(recv,))
    kp, vp, qp = call(
        stack_pairs,
        [((2 * BLK, HD), BF16)] * 3,
        (k, near(k, "zh"), v, far(v, "zh"), q, near(q, "x")),
        smem=0,
    )
    (rows,) = call(stack_two, [((TILE, 2048), BF16)], (rows, near(rows, "y")), smem=0, after=(kp,))
    kf, vn, qf, rows_far = far(kp, "zh"), near(vp, "zh"), far(qp, "x"), far(rows, "y")

    packs = call(
        forward,
        [((HD + 16, BLK), BF16)] * 4,
        (pos, tile_mask, kp, kf, vp, vn, qp, qf),
        flops=2 * kv_mm,
        smem=2,
    )
    packs = [packs[0], near(packs[1], "x"), far(packs[2], "x"), opposite(packs[3], "x")]

    cot, cot_far = call(join_rows, [((TILE, 2048), BF16)] * 2, (pos, rows, rows_far))
    (grads,) = call(
        back_project,
        [((HD, BLK), BF16)],
        (pos, out_weight, cot, cot_far),
        flops=2 * HD * BLK * 2048,
    )
    att, stats, gw_keep, gw_send = call(
        attend,
        [((HD, BLK), BF16), ((16, BLK), BF16)] + [((HD, 1024), F32)] * 2,
        (pos, *packs, grads, cot, cot_far),
        flops=2 * HD * BLK * 2048,
    )
    gw_recv = over_core(gw_send)
    cuts = call(
        weight_cut, [((2 * HD + 16, BLK), BF16)] * 4, (pos, gw_keep, gw_recv, grads, stats)
    )
    cuts = [cuts[0], near(cuts[1], "x"), far(cuts[2], "x"), opposite(cuts[3], "x")]
    att_far = over_pair(att[:, TILE:])
    mixed, mixed_far = call(
        mix,
        [((64, 2048), BF16)] * 2,
        (pos, att, att_far, out_weight),
        flops=2 * TILE * 256 * 2048,
        scratch=[pltpu.VMEM((TILE, 2048), BF16)],
    )
    (share,) = call(sum_cuts, [((HD, BLK), BF16)], cuts, smem=0, after=(mixed_far,))

    dk, dk_far, dv, dv_near, dq, dq_far = call(
        backward,
        [((2 * BLK, HD), BF16)] * 4 + [((2 * HD, BLK), BF16)] * 2,
        (pos, tile_mask, kp, kf, vp, vn, qp, qf, *cuts),
        flops=5 * kv_mm,
        scratch=[pltpu.VMEM((4 * BLK, 4 * BLK), BF16)] * 2,
        smem=2,
        after=(share,),
    )
    (near_sum,) = call(
        sum_two, [((HD, BLK), BF16)], (share, near(share, "zh")), smem=0, after=(dq,)
    )
    (done,) = call(sum_two, [((HD, BLK), BF16)], (near_sum, far(near_sum, "zh")), smem=0)
    done_far = over_pair(done)
    dq_far = lax.optimization_barrier((dq_far, near_sum))[0]
    dk_far, dv_near, _ = lax.optimization_barrier((dk_far, dv_near, done_far))

    dq, dq_near = call(sum_split, [((HD, BLK), BF16)] * 2, (dq, far(dq_far, "x")), smem=0)
    mixed, mixed_near = call(
        sum_split, [((32, 2048), BF16)] * 2, (mixed, far(mixed_far, "y")), smem=0, after=(done,)
    )
    (mixed,) = call(sum_two, [((32, 2048), BF16)], (mixed, near(mixed_near, "y")), smem=0)
    (stack,) = call(weight_stack, [((2 * HD, BLK), BF16)], (pos, done, done_far), after=(dq_near,))
    stacks = [stack, near(stack, "x"), far(stack, "x"), opposite(stack, "x")]
    dk, dk_near = call(
        sum_split, [((BLK, HD), BF16)] * 2, (dk, far(dk_far, "zh")), smem=0, after=(stacks[1], mixed)
    )
    dv, dv_far = call(
        sum_split, [((BLK, HD), BF16)] * 2, (dv, near(dv_near, "zh")), smem=0, after=(stacks[1],)
    )
    dq_near = lax.optimization_barrier((dq_near, stacks[1]))[0]
    out_keep, out_send = call(
        gather_grads,
        [((3 * TILE, HD), BF16)] * 2,
        (dk, near(dk_near, "zh"), dv, far(dv_far, "zh"), dq, near(dq_near, "x")),
        smem=0,
    )

    (here,) = call(
        weight_row, [((2 * HD, 1024), BF16)], (pos, *stacks), after=(out_send,)
    )
    grad_q, grad_k, grad_v, grad_weight = call(
        finish,
        [((TILE, 2 * HD), BF16)] * 3 + [((2 * HD, 2048), F32)],
        (
            pos,
            out_keep,
            over_pair(out_send),
            here,
            over_core(here),
        ),
    )
    return (mixed[None], grad_q[None], grad_k[None], grad_v[None], grad_weight)


def solution(mesh):
    mesh = Mesh(mesh.devices.reshape(4, 4, 2, 4, 2), AXES)
    tokens = ("x", "zh", "par")
    rows = P("core", tokens, "y")
    blocks = P("core", (*tokens, "y"), None)
    weight = P("y", None)
    return jax.shard_map(
        on_device,
        mesh=mesh,
        in_specs=(rows, rows, rows, weight, blocks, P()),
        out_specs=(blocks, rows, rows, rows, weight),
        check_vma=False,
    )
```

```python
import functools
import math

import jax
import jax.numpy as jnp
from jax import lax
from jax.experimental import pallas as pl
from jax.experimental.pallas import tpu as pltpu
from jax.sharding import Mesh
from jax.sharding import PartitionSpec as P

HD = 128
TILE = 128
BLK = 256
SCALE = HD ** (-0.5)
LOG2E = math.log2(math.e)
LOW = -1e30
F32 = jnp.float32
BF16 = jnp.bfloat16
AXES = ("x", "zh", "par", "y", "core")
X, ZH, PAR, Y, CORE = range(5)
ORDER = (0, 1, 3, 2)
NN = (((1,), (0,)), ((), ()))
NT = (((1,), (1,)), ((), ()))


def dot(a, b, dims=NN):
    return lax.dot_general(a, b, dims, preferred_element_type=F32)


def call(
    body, outs, ins, flops=0, scratch=(), smem=1, vmem=48, after=(), space=pltpu.VMEM,
    out_space=pltpu.VMEM,
):
    specs = [pl.BlockSpec(memory_space=pltpu.SMEM)] * smem
    specs += [pl.BlockSpec(memory_space=space)] * (len(ins) - smem)
    used = len(ins)
    if after:
        specs += [pl.BlockSpec(memory_space=pl.ANY)] * len(after)
        inner = body

        def body(*refs):
            inner(*refs[:used], *refs[used + len(after) :])

    shapes = [jax.ShapeDtypeStruct(s, d) for s, d in outs]
    moved = sum(math.prod(a.shape) * a.dtype.itemsize for a in list(ins) + shapes)
    ins = tuple(ins) + tuple(after)
    return pl.pallas_call(
        body,
        out_shape=shapes,
        in_specs=specs,
        out_specs=[pl.BlockSpec(memory_space=out_space)] * len(outs),
        scratch_shapes=list(scratch),
        compiler_params=pltpu.CompilerParams(vmem_limit_bytes=vmem * 2**20),
        cost_estimate=pl.CostEstimate(flops=flops, bytes_accessed=moved, transcendentals=0),
    )(*ins)


def own_blocks(keep, recv, k, v, q):
    for n, ref in ((0, q), (1, k), (2, v)):
        rows = slice(n * TILE, (n + 1) * TILE)
        ref[:TILE, :] = keep[rows, :]
        ref[TILE:, :] = recv[rows, :]


def copy_rows(rows, out):
    out[...] = rows[...]


def stack_two(a, b, out):
    rows = a.shape[0]
    out[:rows, :] = a[...]
    out[rows:, :] = b[...]


def stack_pairs(k0, k1, v0, v1, q0, q1, k, v, q):
    stack_two(k0, k1, k)
    stack_two(v0, v1, v)
    stack_two(q0, q1, q)


def join_rows(pos, pair, other, near, far):
    for n in range(4):
        ref = (pair, other)[n // 2]
        start = (n % 2) * 64
        rows = pl.ds(pl.multiple_of((pos[Y] ^ ORDER[n]) * 32, 32), 32)
        near[rows, :] = ref[start : start + 32, :]
        far[rows, :] = ref[start + 32 : start + 64, :]


def bias_rows(pos, mask, query_x):
    lane = lax.broadcasted_iota(jnp.int32, (1, BLK), 1)
    par = pos[PAR]
    query = (query_x * 4 + pos[ZH]) * 2
    rows = []
    for e in ORDER:
        key = (pos[X] * 4 + (pos[ZH] ^ e)) * 2
        for tile in (par, 1 - par):
            near = jnp.where(mask[query + par, key + tile] > 0, 0.0, LOW)
            far = jnp.where(mask[query + 1 - par, key + tile] > 0, 0.0, LOW)
            rows.append(jnp.where(lane < TILE, near, far))
    return rows


def scores_of(keys, queries, rows):
    raw = dot(keys, queries, NT) * (SCALE * LOG2E)
    return jnp.concatenate(
        [raw[t * TILE : (t + 1) * TILE] + row for t, row in enumerate(rows)], axis=0
    )


def split3(value):
    high = value.astype(BF16).astype(F32)
    rest = value - high
    middle = rest.astype(BF16).astype(F32)
    low = (rest - middle).astype(BF16).astype(F32)
    return high, middle, low


def pack_rows(values):
    row = lax.broadcasted_iota(jnp.int32, (16, BLK), 0)
    packed = jnp.zeros((16, BLK), F32)
    for n, value in enumerate(values):
        packed = jnp.where(row == n, value, packed)
    return packed.astype(BF16)


def load_kv(kp, kf, vp, vn):
    keys = jnp.concatenate([kp[...], kf[...]], axis=0)
    values = [vp[:BLK, :], vn[:BLK, :], vp[BLK:, :], vn[BLK:, :]]
    return keys, jnp.concatenate(values, axis=0)


def transposed(a):
    return a.astype(F32).T.astype(BF16)


def query_block(qp, qf, n):
    return (qp, qf)[n // 2][(n % 2) * BLK : (n % 2 + 1) * BLK, :]


def forward(pos, mask, kp, kf, vp, vn, qp, qf, p0, p1, p2, p3):
    keys, values = load_kv(kp, kf, vp, vn)
    values_t = transposed(values)
    for n, pack in enumerate((p0, p1, p2, p3)):
        rows = bias_rows(pos, mask, pos[X] ^ ORDER[n])
        queries = query_block(qp, qf, n)
        scores = [
            scores_of(keys[e * BLK : (e + 1) * BLK], queries, rows[2 * e : 2 * e + 2])
            for e in range(4)
        ]
        largest = functools.reduce(
            jnp.maximum, [jnp.max(block, axis=0, keepdims=True) for block in scores]
        )
        largest = jnp.maximum(largest, 0.1 * LOW)
        total = jnp.zeros((1, BLK), F32)
        summed = jnp.zeros((HD, BLK), F32)
        for e in range(4):
            weights = jnp.exp2(scores[e] - largest)
            total = total + jnp.sum(weights, axis=0, keepdims=True)
            summed = summed + dot(values_t[:, e * BLK : (e + 1) * BLK], weights.astype(BF16))
        some = total > 0.0
        safe = jnp.where(some, total, 1.0)
        pack[:HD, :] = (summed / safe).astype(BF16)
        pack[HD:, :] = pack_rows(split3(jnp.where(some, largest + jnp.log2(safe), LOW)))


def backward(
    pos, mask, kp, kf, vp, vn, qp, qf, s0, s1, s2, s3,
    dk, dk_far, dv, dv_near, dq, dq_far, probs_of, scores_grad_of,
):
    keys, values = load_kv(kp, kf, vp, vn)
    keys_t = transposed(keys)
    for n, ref in enumerate((s0, s1, s2, s3)):
        rows = bias_rows(pos, mask, pos[X] ^ ORDER[n])
        s = ref[2 * HD :, :].astype(F32)
        lse = s[0:1] + s[1:2] + s[2:3]
        delta = s[3:4] + s[4:5] + s[5:6]
        probs = jnp.exp2(scores_of(keys, query_block(qp, qf, n), rows) - lse)
        grad_probs = dot(values, ref[HD : 2 * HD, :])
        grad_scores = (probs * (grad_probs - delta)).astype(BF16)
        columns = slice(n * BLK, (n + 1) * BLK)
        probs_of[:, columns] = probs.astype(BF16)
        scores_grad_of[:, columns] = grad_scores
        out = (dq, dq_far)[n // 2]
        out[(n % 2) * HD : (n % 2 + 1) * HD, :] = (dot(keys_t, grad_scores) * SCALE).astype(BF16)
    queries = jnp.concatenate([qp[...], qf[...]], axis=0)
    grads = jnp.concatenate([ref[HD : 2 * HD, :] for ref in (s0, s1, s2, s3)], axis=1)
    for n in range(4):
        block = slice(n * BLK, (n + 1) * BLK)
        half = slice((n % 2) * BLK, (n % 2 + 1) * BLK)
        out = (dk, dk_far)[n // 2]
        out[half, :] = (dot(scores_grad_of[block, :], queries) * SCALE).astype(BF16)
        half = slice((n // 2) * BLK, (n // 2 + 1) * BLK)
        out = (dv, dv_near)[n % 2]
        out[half, :] = dot(probs_of[block, :], grads, NT).astype(BF16)


def back_project(pos, w, near, far, grads):
    head = w[pl.ds(pl.multiple_of(pos[PAR] * HD, HD), HD), :]
    grads[:, :TILE] = dot(head, near[...], NT).astype(BF16)
    grads[:, TILE:] = dot(head, far[...], NT).astype(BF16)


def attend(pos, p0, p1, p2, p3, grads, near, far, att, stats, keep, send):
    lses, parts = [], []
    for pack in (p0, p1, p2, p3):
        parts.append(pack[:HD, :].astype(F32))
        s = pack[HD:, :].astype(F32)
        lses.append(s[0:1] + s[1:2] + s[2:3])
    largest = functools.reduce(jnp.maximum, lses)
    weights = [jnp.exp2(v - largest) for v in lses]
    total = sum(weights)
    out = sum((w / total) * p for w, p in zip(weights, parts)).astype(BF16)
    att[...] = out
    delta = jnp.sum(grads[...].astype(F32) * out.astype(F32), axis=0, keepdims=True)
    stats[...] = pack_rows(split3(largest + jnp.log2(total)) + split3(delta))
    both = dot(out[:, :TILE], near[...]) + dot(out[:, TILE:], far[...])

    @pl.when(pos[CORE] == 0)
    def _():
        keep[...] = both[:, :1024]
        send[...] = both[:, 1024:].astype(BF16)

    @pl.when(pos[CORE] != 0)
    def _():
        keep[...] = both[:, 1024:]
        send[...] = both[:, :1024].astype(BF16)


def weight_cut(pos, mine, other, grads, stats, b0, b1, b2, b3):
    for n, ref in enumerate((b0, b1, b2, b3)):
        columns = pl.ds(pl.multiple_of((pos[X] ^ ORDER[n]) * BLK, BLK), BLK)
        ref[:HD, :] = (mine[:, columns] + other[:, columns].astype(F32)).astype(BF16)
        ref[HD : 2 * HD, :] = grads[...]
        ref[2 * HD :, :] = stats[...]


def add(a, b):
    return a.astype(F32) + b.astype(F32)


def sum_cuts(a, b, c, d, out):
    out[...] = (add(a[:HD, :], b[:HD, :]) + add(c[:HD, :], d[:HD, :])).astype(BF16)


def sum_two(a, b, out):
    out[...] = add(a[...], b[...]).astype(BF16)


def sum_split(a, b, keep, send):
    total = add(a[...], b[...]).astype(BF16)
    rows = keep.shape[0]
    keep[...] = total[:rows]
    send[...] = total[rows:]


def weight_stack(pos, mine, other, out):
    out[pl.ds(pl.multiple_of(pos[PAR] * HD, HD), HD), :] = mine[...]
    out[pl.ds(pl.multiple_of((1 - pos[PAR]) * HD, HD), HD), :] = other[...]


def weight_row(pos, f0, f1, f2, f3, out):
    for n, ref in enumerate((f0, f1, f2, f3)):
        columns = pl.ds(pl.multiple_of((pos[X] ^ ORDER[n]) * BLK, BLK), BLK)
        out[:, columns] = ref[...]


def mix(pos, att, other, w, out, out_far, full):
    mine_rows = pl.ds(pl.multiple_of(pos[PAR] * HD, HD), HD)
    other_rows = pl.ds(pl.multiple_of((1 - pos[PAR]) * HD, HD), HD)
    mine_t = att[:, :TILE].astype(F32).T.astype(BF16)
    other_t = other[...].astype(F32).T.astype(BF16)
    full[...] = (dot(mine_t, w[mine_rows, :]) + dot(other_t, w[other_rows, :])).astype(BF16)
    for n in range(4):
        rows = pl.ds(pl.multiple_of((pos[Y] ^ ORDER[n]) * 32, 32), 32)
        (out, out_far)[n // 2][(n % 2) * 32 : (n % 2 + 1) * 32, :] = full[rows, :]


def gather_grads(k, k_near, v, v_far, q, q_near, keep, send):
    q = add(q[...], q_near[...])
    keep[:TILE, :] = q[:, :TILE].T.astype(BF16)
    send[:TILE, :] = q[:, TILE:].T.astype(BF16)
    for n, (mine, other) in enumerate(((k, k_near), (v, v_far))):
        total = add(mine[...], other[...]).astype(BF16)
        rows = slice((n + 1) * TILE, (n + 2) * TILE)
        keep[rows, :] = total[:TILE]
        send[rows, :] = total[TILE:]


def finish(
    pos, mine, other, here, core, mix_mine, mix_other, q, k, v, weight, mixed,
    heads, halves, rows_out, sems,
):
    copies = []
    for n, (half, ref) in enumerate(((pos[CORE], here), (1 - pos[CORE], core))):
        halves[n] = ref[...].astype(F32)
        columns = pl.ds(pl.multiple_of(half * 1024, 1024), 1024)
        copies.append(pltpu.make_async_copy(halves.at[n], weight.at[:, columns], sems.at[n]))
        copies[-1].start()
    left = pl.ds(pl.multiple_of(pos[PAR] * HD, HD), HD)
    right = pl.ds(pl.multiple_of((1 - pos[PAR]) * HD, HD), HD)
    for n, ref in enumerate((q, k, v)):
        rows = slice(n * TILE, (n + 1) * TILE)
        heads[n, :, left] = mine[rows, :]
        heads[n, :, right] = other[rows, :]
        copies.append(pltpu.make_async_copy(heads.at[n], ref, sems.at[2 + n]))
        copies[-1].start()
    rows_out[...] = add(mix_mine[...], mix_other[...]).astype(BF16)
    copies.append(pltpu.make_async_copy(rows_out, mixed, sems.at[5]))
    copies[-1].start()
    for copy in copies:
        copy.wait()


def near(a, axis):
    return lax.ppermute(a, axis, [(0, 1), (1, 0), (2, 3), (3, 2)])


def far(a, axis):
    return lax.ppermute(a, axis, [(0, 3), (3, 0), (1, 2), (2, 1)])


def opposite(a, axis):
    return lax.ppermute(a, axis, [(0, 2), (2, 0), (1, 3), (3, 1)])


def over_pair(a):
    return lax.ppermute(a, "par", [(0, 1), (1, 0)])


def over_core(a):
    return lax.ppermute(a, "core", [(0, 1), (1, 0)])


def on_device(query_rows, key_rows, value_rows, out_weight, cotangent, tile_mask):
    pos = jnp.stack([lax.axis_index(name) for name in AXES]).astype(jnp.int32)
    kv_mm = 2 * 1024 * 1024 * HD

    inputs = (query_rows[0], key_rows[0], value_rows[0])
    first = pos[PAR] == 0
    send = jnp.concatenate([jnp.where(first, rows[:, HD:], rows[:, :HD]) for rows in inputs])
    keep = jnp.concatenate([jnp.where(first, rows[:, :HD], rows[:, HD:]) for rows in inputs])
    recv = over_pair(send)
    rows_far = over_pair(cotangent[0])
    (rows,) = call(copy_rows, [((32, 2048), BF16)], (cotangent[0],), smem=0, after=(send,))
    k, v, q = call(own_blocks, [((BLK, HD), BF16)] * 3, (keep, recv), smem=0)
    (rows,) = call(stack_two, [((64, 2048), BF16)], (rows, rows_far), smem=0, after=(recv,))
    kp, vp, qp = call(
        stack_pairs,
        [((2 * BLK, HD), BF16)] * 3,
        (k, near(k, "zh"), v, far(v, "zh"), q, near(q, "x")),
        smem=0,
    )
    (rows,) = call(stack_two, [((TILE, 2048), BF16)], (rows, near(rows, "y")), smem=0, after=(kp,))
    kf, vn, qf, rows_far = far(kp, "zh"), near(vp, "zh"), far(qp, "x"), far(rows, "y")

    packs = call(
        forward,
        [((HD + 16, BLK), BF16)] * 4,
        (pos, tile_mask, kp, kf, vp, vn, qp, qf),
        flops=2 * kv_mm,
        smem=2,
    )
    packs = [packs[0], near(packs[1], "x"), far(packs[2], "x"), opposite(packs[3], "x")]

    cot, cot_far = call(join_rows, [((TILE, 2048), BF16)] * 2, (pos, rows, rows_far))
    (grads,) = call(
        back_project,
        [((HD, BLK), BF16)],
        (pos, out_weight, cot, cot_far),
        flops=2 * HD * BLK * 2048,
    )
    att, stats, gw_keep, gw_send = call(
        attend,
        [((HD, BLK), BF16), ((16, BLK), BF16), ((HD, 1024), F32), ((HD, 1024), BF16)],
        (pos, *packs, grads, cot, cot_far),
        flops=2 * HD * BLK * 2048,
    )
    gw_recv = over_core(gw_send)
    cuts = call(
        weight_cut, [((2 * HD + 16, BLK), BF16)] * 4, (pos, gw_keep, gw_recv, grads, stats)
    )
    cuts = [cuts[0], near(cuts[1], "x"), far(cuts[2], "x"), opposite(cuts[3], "x")]
    att_far = over_pair(att[:, TILE:])
    mixed, mixed_far = call(
        mix,
        [((64, 2048), BF16)] * 2,
        (pos, att, att_far, out_weight),
        flops=2 * TILE * 256 * 2048,
        scratch=[pltpu.VMEM((TILE, 2048), BF16)],
    )
    (share,) = call(sum_cuts, [((HD, BLK), BF16)], cuts, smem=0, after=(mixed_far,))

    dk, dk_far, dv, dv_near, dq, dq_far = call(
        backward,
        [((2 * BLK, HD), BF16)] * 4 + [((2 * HD, BLK), BF16)] * 2,
        (pos, tile_mask, kp, kf, vp, vn, qp, qf, *cuts),
        flops=5 * kv_mm,
        scratch=[pltpu.VMEM((4 * BLK, 4 * BLK), BF16)] * 2,
        smem=2,
        after=(share,),
    )
    (near_sum,) = call(
        sum_two, [((HD, BLK), BF16)], (share, near(share, "zh")), smem=0, after=(dq,)
    )
    (done,) = call(sum_two, [((HD, BLK), BF16)], (near_sum, far(near_sum, "zh")), smem=0)
    done_far = over_pair(done)
    dq_far = lax.optimization_barrier((dq_far, near_sum))[0]
    dk_far, dv_near, _ = lax.optimization_barrier((dk_far, dv_near, done))

    dq, dq_near = call(sum_split, [((HD, BLK), BF16)] * 2, (dq, far(dq_far, "x")), smem=0)
    mixed, mixed_near = call(
        sum_split, [((32, 2048), BF16)] * 2, (mixed, far(mixed_far, "y")), smem=0, after=(done,)
    )
    mixed_other = near(mixed_near, "y")
    (stack,) = call(weight_stack, [((2 * HD, BLK), BF16)], (pos, done, done_far), after=(dq_near,))
    stacks = [stack, near(stack, "x"), far(stack, "x"), opposite(stack, "x")]
    dk, dk_near = call(
        sum_split, [((BLK, HD), BF16)] * 2, (dk, far(dk_far, "zh")), smem=0, after=(mixed_other,)
    )
    dv, dv_far = call(
        sum_split, [((BLK, HD), BF16)] * 2, (dv, near(dv_near, "zh")), smem=0
    )
    dq_near = lax.optimization_barrier((dq_near, stacks[1]))[0]
    out_keep, out_send = call(
        gather_grads,
        [((3 * TILE, HD), BF16)] * 2,
        (dk, near(dk_near, "zh"), dv, far(dv_far, "zh"), dq, near(dq_near, "x")),
        smem=0,
    )

    (here,) = call(
        weight_row, [((2 * HD, 1024), BF16)], (pos, *stacks), after=(out_send,)
    )
    grad_q, grad_k, grad_v, grad_weight, mixed = call(
        finish,
        [((TILE, 2 * HD), BF16)] * 3 + [((2 * HD, 2048), F32), ((32, 2048), BF16)],
        (
            pos,
            out_keep,
            over_pair(out_send),
            here,
            over_core(here),
            mixed,
            mixed_other,
        ),
        scratch=[
            pltpu.VMEM((3, TILE, 2 * HD), BF16),
            pltpu.VMEM((2, 2 * HD, 1024), F32),
            pltpu.VMEM((32, 2048), BF16),
            pltpu.SemaphoreType.DMA((6,)),
        ],
        out_space=pl.ANY,
    )
    return (mixed[None], grad_q[None], grad_k[None], grad_v[None], grad_weight)


def solution(mesh):
    mesh = Mesh(mesh.devices.reshape(4, 4, 2, 4, 2), AXES)
    tokens = ("x", "zh", "par")
    rows = P("core", tokens, "y")
    blocks = P("core", (*tokens, "y"), None)
    weight = P("y", None)
    return jax.shard_map(
        on_device,
        mesh=mesh,
        in_specs=(rows, rows, rows, weight, blocks, P()),
        out_specs=(blocks, rows, rows, rows, weight),
        check_vma=False,
    )
```

```python
import functools
import math

import jax
import jax.numpy as jnp
from jax import lax
from jax.experimental import pallas as pl
from jax.experimental.pallas import tpu as pltpu
from jax.sharding import Mesh
from jax.sharding import PartitionSpec as P

HD = 128
TILE = 128
BLK = 256
SCALE = HD ** (-0.5)
LOG2E = math.log2(math.e)
LOW = -1e30
F32 = jnp.float32
BF16 = jnp.bfloat16
AXES = ("x", "zh", "par", "y", "core")
X, ZH, PAR, Y, CORE = range(5)
ORDER = (0, 1, 3, 2)
NN = (((1,), (0,)), ((), ()))
NT = (((1,), (1,)), ((), ()))


def dot(a, b, dims=NN):
    return lax.dot_general(a, b, dims, preferred_element_type=F32)


def call(
    body, outs, ins, flops=0, scratch=(), smem=1, vmem=48, after=(), space=pltpu.VMEM,
    out_space=pltpu.VMEM,
):
    specs = [pl.BlockSpec(memory_space=pltpu.SMEM)] * smem
    specs += [pl.BlockSpec(memory_space=space)] * (len(ins) - smem)
    used = len(ins)
    out_spaces = out_space if isinstance(out_space, list) else [out_space] * len(outs)
    if after:
        specs += [pl.BlockSpec(memory_space=pl.ANY)] * len(after)
        inner = body

        def body(*refs):
            inner(*refs[:used], *refs[used + len(after) :])

    shapes = [jax.ShapeDtypeStruct(s, d) for s, d in outs]
    moved = sum(math.prod(a.shape) * a.dtype.itemsize for a in list(ins) + shapes)
    ins = tuple(ins) + tuple(after)
    return pl.pallas_call(
        body,
        out_shape=shapes,
        in_specs=specs,
        out_specs=[pl.BlockSpec(memory_space=place) for place in out_spaces],
        scratch_shapes=list(scratch),
        compiler_params=pltpu.CompilerParams(vmem_limit_bytes=vmem * 2**20),
        cost_estimate=pl.CostEstimate(flops=flops, bytes_accessed=moved, transcendentals=0),
    )(*ins)


def own_blocks(keep, recv, k, v, q):
    for n, ref in ((0, q), (1, k), (2, v)):
        rows = slice(n * TILE, (n + 1) * TILE)
        ref[:TILE, :] = keep[rows, :]
        ref[TILE:, :] = recv[rows, :]


def copy_rows(rows, out):
    out[...] = rows[...]


def stack_two(a, b, out):
    rows = a.shape[0]
    out[:rows, :] = a[...]
    out[rows:, :] = b[...]


def stack_pairs(k0, k1, v0, v1, q0, q1, k, v, q):
    stack_two(k0, k1, k)
    stack_two(v0, v1, v)
    stack_two(q0, q1, q)


def join_rows(pos, pair, other, near, far):
    for n in range(4):
        ref = (pair, other)[n // 2]
        start = (n % 2) * 64
        rows = pl.ds(pl.multiple_of((pos[Y] ^ ORDER[n]) * 32, 32), 32)
        near[rows, :] = ref[start : start + 32, :]
        far[rows, :] = ref[start + 32 : start + 64, :]


def bias_rows(pos, mask, query_x):
    lane = lax.broadcasted_iota(jnp.int32, (1, BLK), 1)
    par = pos[PAR]
    query = (query_x * 4 + pos[ZH]) * 2
    rows = []
    for e in ORDER:
        key = (pos[X] * 4 + (pos[ZH] ^ e)) * 2
        for tile in (par, 1 - par):
            near = jnp.where(mask[query + par, key + tile] > 0, 0.0, LOW)
            far = jnp.where(mask[query + 1 - par, key + tile] > 0, 0.0, LOW)
            rows.append(jnp.where(lane < TILE, near, far))
    return rows


def scores_of(keys, queries, rows):
    raw = dot(keys, queries, NT) * (SCALE * LOG2E)
    return jnp.concatenate(
        [raw[t * TILE : (t + 1) * TILE] + row for t, row in enumerate(rows)], axis=0
    )


def split3(value):
    high = value.astype(BF16).astype(F32)
    rest = value - high
    middle = rest.astype(BF16).astype(F32)
    low = (rest - middle).astype(BF16).astype(F32)
    return high, middle, low


def pack_rows(values):
    row = lax.broadcasted_iota(jnp.int32, (16, BLK), 0)
    packed = jnp.zeros((16, BLK), F32)
    for n, value in enumerate(values):
        packed = jnp.where(row == n, value, packed)
    return packed.astype(BF16)


def load_kv(kp, kf, vp, vn):
    keys = jnp.concatenate([kp[...], kf[...]], axis=0)
    values = [vp[:BLK, :], vn[:BLK, :], vp[BLK:, :], vn[BLK:, :]]
    return keys, jnp.concatenate(values, axis=0)


def transposed(a):
    return a.astype(F32).T.astype(BF16)


def query_block(qp, qf, n):
    return (qp, qf)[n // 2][(n % 2) * BLK : (n % 2 + 1) * BLK, :]


def forward(pos, mask, kp, kf, vp, vn, qp, qf, p0, p1, p2, p3):
    keys, values = load_kv(kp, kf, vp, vn)
    values_t = transposed(values)
    for n, pack in enumerate((p0, p1, p2, p3)):
        rows = bias_rows(pos, mask, pos[X] ^ ORDER[n])
        queries = query_block(qp, qf, n)
        scores = [
            scores_of(keys[e * BLK : (e + 1) * BLK], queries, rows[2 * e : 2 * e + 2])
            for e in range(4)
        ]
        largest = functools.reduce(
            jnp.maximum, [jnp.max(block, axis=0, keepdims=True) for block in scores]
        )
        largest = jnp.maximum(largest, 0.1 * LOW)
        total = jnp.zeros((1, BLK), F32)
        summed = jnp.zeros((HD, BLK), F32)
        for e in range(4):
            weights = jnp.exp2(scores[e] - largest)
            total = total + jnp.sum(weights, axis=0, keepdims=True)
            summed = summed + dot(values_t[:, e * BLK : (e + 1) * BLK], weights.astype(BF16))
        some = total > 0.0
        safe = jnp.where(some, total, 1.0)
        pack[:HD, :] = (summed / safe).astype(BF16)
        pack[HD:, :] = pack_rows(split3(jnp.where(some, largest + jnp.log2(safe), LOW)))


def backward(
    pos, mask, kp, kf, vp, vn, qp, qf, s0, s1, s2, s3,
    dk, dk_far, dv, dv_near, dq, dq_far, probs_of, scores_grad_of,
):
    keys, values = load_kv(kp, kf, vp, vn)
    keys_t = transposed(keys)
    for n, ref in enumerate((s0, s1, s2, s3)):
        rows = bias_rows(pos, mask, pos[X] ^ ORDER[n])
        s = ref[2 * HD :, :].astype(F32)
        lse = s[0:1] + s[1:2] + s[2:3]
        delta = s[3:4] + s[4:5] + s[5:6]
        probs = jnp.exp2(scores_of(keys, query_block(qp, qf, n), rows) - lse)
        grad_probs = dot(values, ref[HD : 2 * HD, :])
        grad_scores = (probs * (grad_probs - delta)).astype(BF16)
        columns = slice(n * BLK, (n + 1) * BLK)
        probs_of[:, columns] = probs.astype(BF16)
        scores_grad_of[:, columns] = grad_scores
        out = (dq, dq_far)[n // 2]
        out[(n % 2) * HD : (n % 2 + 1) * HD, :] = (dot(keys_t, grad_scores) * SCALE).astype(BF16)
    queries = jnp.concatenate([qp[...], qf[...]], axis=0)
    grads = jnp.concatenate([ref[HD : 2 * HD, :] for ref in (s0, s1, s2, s3)], axis=1)
    for n in range(4):
        block = slice(n * BLK, (n + 1) * BLK)
        half = slice((n % 2) * BLK, (n % 2 + 1) * BLK)
        out = (dk, dk_far)[n // 2]
        out[half, :] = (dot(scores_grad_of[block, :], queries) * SCALE).astype(BF16)
        half = slice((n // 2) * BLK, (n // 2 + 1) * BLK)
        out = (dv, dv_near)[n % 2]
        out[half, :] = dot(probs_of[block, :], grads, NT).astype(BF16)


def back_project(pos, w, near, far, grads):
    head = w[pl.ds(pl.multiple_of(pos[PAR] * HD, HD), HD), :]
    grads[:, :TILE] = dot(head, near[...], NT).astype(BF16)
    grads[:, TILE:] = dot(head, far[...], NT).astype(BF16)


def attend(pos, p0, p1, p2, p3, grads, near, far, att, stats, keep, send):
    lses, parts = [], []
    for pack in (p0, p1, p2, p3):
        parts.append(pack[:HD, :].astype(F32))
        s = pack[HD:, :].astype(F32)
        lses.append(s[0:1] + s[1:2] + s[2:3])
    largest = functools.reduce(jnp.maximum, lses)
    weights = [jnp.exp2(v - largest) for v in lses]
    total = sum(weights)
    out = sum((w / total) * p for w, p in zip(weights, parts)).astype(BF16)
    att[...] = out
    delta = jnp.sum(grads[...].astype(F32) * out.astype(F32), axis=0, keepdims=True)
    stats[...] = pack_rows(split3(largest + jnp.log2(total)) + split3(delta))
    both = dot(out[:, :TILE], near[...]) + dot(out[:, TILE:], far[...])

    @pl.when(pos[CORE] == 0)
    def _():
        keep[...] = both[:, :1024]
        send[...] = both[:, 1024:].astype(BF16)

    @pl.when(pos[CORE] != 0)
    def _():
        keep[...] = both[:, 1024:]
        send[...] = both[:, :1024].astype(BF16)


def weight_cut(pos, mine, other, grads, stats, b0, b1, b2, b3):
    for n, ref in enumerate((b0, b1, b2, b3)):
        columns = pl.ds(pl.multiple_of((pos[X] ^ ORDER[n]) * BLK, BLK), BLK)
        ref[:HD, :] = (mine[:, columns] + other[:, columns].astype(F32)).astype(BF16)
        ref[HD : 2 * HD, :] = grads[...]
        ref[2 * HD :, :] = stats[...]


def add(a, b):
    return a.astype(F32) + b.astype(F32)


def sum_cuts(a, b, c, d, out):
    out[...] = (add(a[:HD, :], b[:HD, :]) + add(c[:HD, :], d[:HD, :])).astype(BF16)


def sum_two(a, b, out):
    out[...] = add(a[...], b[...]).astype(BF16)


def sum_split(a, b, keep, send):
    total = add(a[...], b[...]).astype(BF16)
    rows = keep.shape[0]
    keep[...] = total[:rows]
    send[...] = total[rows:]


def weight_stack(pos, mine, other, out):
    out[pl.ds(pl.multiple_of(pos[PAR] * HD, HD), HD), :] = mine[...]
    out[pl.ds(pl.multiple_of((1 - pos[PAR]) * HD, HD), HD), :] = other[...]


def weight_row(pos, f0, f1, f2, f3, out):
    for n, ref in enumerate((f0, f1, f2, f3)):
        columns = pl.ds(pl.multiple_of((pos[X] ^ ORDER[n]) * BLK, BLK), BLK)
        out[:, columns] = ref[...]


def mix(pos, att, other, w, out, out_far, full):
    mine_rows = pl.ds(pl.multiple_of(pos[PAR] * HD, HD), HD)
    other_rows = pl.ds(pl.multiple_of((1 - pos[PAR]) * HD, HD), HD)
    mine_t = att[:, :TILE].astype(F32).T.astype(BF16)
    other_t = other[...].astype(F32).T.astype(BF16)
    full[...] = (dot(mine_t, w[mine_rows, :]) + dot(other_t, w[other_rows, :])).astype(BF16)
    for n in range(4):
        rows = pl.ds(pl.multiple_of((pos[Y] ^ ORDER[n]) * 32, 32), 32)
        (out, out_far)[n // 2][(n % 2) * 32 : (n % 2 + 1) * 32, :] = full[rows, :]


def gather_grads(k, k_near, v, v_far, q, q_near, keep, send):
    q = add(q[...], q_near[...])
    keep[:TILE, :] = q[:, :TILE].T.astype(BF16)
    send[:TILE, :] = q[:, TILE:].T.astype(BF16)
    for n, (mine, other) in enumerate(((k, k_near), (v, v_far))):
        total = add(mine[...], other[...]).astype(BF16)
        rows = slice((n + 1) * TILE, (n + 2) * TILE)
        keep[rows, :] = total[:TILE]
        send[rows, :] = total[TILE:]


def weight_out(pos, here, core, mix_mine, mix_other, weight, mixed, flag, halves, rows_out, sems):
    copies = []
    flag[...] = jnp.zeros_like(flag)
    for n, (half, ref) in enumerate(((pos[CORE], here), (1 - pos[CORE], core))):
        halves[n] = ref[...].astype(F32)
        columns = pl.ds(pl.multiple_of(half * 1024, 1024), 1024)
        copies.append(pltpu.make_async_copy(halves.at[n], weight.at[:, columns], sems.at[n]))
        copies[-1].start()
    rows_out[...] = add(mix_mine[...], mix_other[...]).astype(BF16)
    copies.append(pltpu.make_async_copy(rows_out, mixed, sems.at[2]))
    copies[-1].start()
    for copy in copies:
        copy.wait()


def join_heads(pos, mine, other, q, k, v, heads, sems):
    left = pl.ds(pl.multiple_of(pos[PAR] * HD, HD), HD)
    right = pl.ds(pl.multiple_of((1 - pos[PAR]) * HD, HD), HD)
    copies = []
    for n, ref in enumerate((q, k, v)):
        rows = slice(n * TILE, (n + 1) * TILE)
        heads[n, :, left] = mine[rows, :]
        heads[n, :, right] = other[rows, :]
        copies.append(pltpu.make_async_copy(heads.at[n], ref, sems.at[n]))
        copies[-1].start()
    for copy in copies:
        copy.wait()


def near(a, axis):
    return lax.ppermute(a, axis, [(0, 1), (1, 0), (2, 3), (3, 2)])


def far(a, axis):
    return lax.ppermute(a, axis, [(0, 3), (3, 0), (1, 2), (2, 1)])


def opposite(a, axis):
    return lax.ppermute(a, axis, [(0, 2), (2, 0), (1, 3), (3, 1)])


def over_pair(a):
    return lax.ppermute(a, "par", [(0, 1), (1, 0)])


def over_core(a):
    return lax.ppermute(a, "core", [(0, 1), (1, 0)])


def on_device(query_rows, key_rows, value_rows, out_weight, cotangent, tile_mask):
    pos = jnp.stack([lax.axis_index(name) for name in AXES]).astype(jnp.int32)
    kv_mm = 2 * 1024 * 1024 * HD

    inputs = (query_rows[0], key_rows[0], value_rows[0])
    first = pos[PAR] == 0
    send = jnp.concatenate([jnp.where(first, rows[:, HD:], rows[:, :HD]) for rows in inputs])
    keep = jnp.concatenate([jnp.where(first, rows[:, :HD], rows[:, HD:]) for rows in inputs])
    recv = over_pair(send)
    rows_far = over_pair(cotangent[0])
    (rows,) = call(copy_rows, [((32, 2048), BF16)], (cotangent[0],), smem=0, after=(send,))
    k, v, q = call(own_blocks, [((BLK, HD), BF16)] * 3, (keep, recv), smem=0)
    (rows,) = call(stack_two, [((64, 2048), BF16)], (rows, rows_far), smem=0, after=(recv,))
    kp, vp, qp = call(
        stack_pairs,
        [((2 * BLK, HD), BF16)] * 3,
        (k, near(k, "zh"), v, far(v, "zh"), q, near(q, "x")),
        smem=0,
    )
    (rows,) = call(stack_two, [((TILE, 2048), BF16)], (rows, near(rows, "y")), smem=0, after=(kp,))
    kf, vn, qf, rows_far = far(kp, "zh"), near(vp, "zh"), far(qp, "x"), far(rows, "y")

    packs = call(
        forward,
        [((HD + 16, BLK), BF16)] * 4,
        (pos, tile_mask, kp, kf, vp, vn, qp, qf),
        flops=2 * kv_mm,
        smem=2,
    )
    packs = [packs[0], near(packs[1], "x"), far(packs[2], "x"), opposite(packs[3], "x")]

    cot, cot_far = call(join_rows, [((TILE, 2048), BF16)] * 2, (pos, rows, rows_far))
    (grads,) = call(
        back_project,
        [((HD, BLK), BF16)],
        (pos, out_weight, cot, cot_far),
        flops=2 * HD * BLK * 2048,
    )
    att, stats, gw_keep, gw_send = call(
        attend,
        [((HD, BLK), BF16), ((16, BLK), BF16), ((HD, 1024), F32), ((HD, 1024), BF16)],
        (pos, *packs, grads, cot, cot_far),
        flops=2 * HD * BLK * 2048,
    )
    gw_recv = over_core(gw_send)
    cuts = call(
        weight_cut, [((2 * HD + 16, BLK), BF16)] * 4, (pos, gw_keep, gw_recv, grads, stats)
    )
    cuts = [cuts[0], near(cuts[1], "x"), far(cuts[2], "x"), opposite(cuts[3], "x")]
    att_far = over_pair(att[:, TILE:])
    mixed, mixed_far = call(
        mix,
        [((64, 2048), BF16)] * 2,
        (pos, att, att_far, out_weight),
        flops=2 * TILE * 256 * 2048,
        scratch=[pltpu.VMEM((TILE, 2048), BF16)],
    )
    (share,) = call(sum_cuts, [((HD, BLK), BF16)], cuts, smem=0, after=(mixed_far,))

    dk, dk_far, dv, dv_near, dq, dq_far = call(
        backward,
        [((2 * BLK, HD), BF16)] * 4 + [((2 * HD, BLK), BF16)] * 2,
        (pos, tile_mask, kp, kf, vp, vn, qp, qf, *cuts),
        flops=5 * kv_mm,
        scratch=[pltpu.VMEM((4 * BLK, 4 * BLK), BF16)] * 2,
        smem=2,
        after=(share,),
    )
    (near_sum,) = call(
        sum_two, [((HD, BLK), BF16)], (share, near(share, "zh")), smem=0, after=(dq,)
    )
    (done,) = call(sum_two, [((HD, BLK), BF16)], (near_sum, far(near_sum, "zh")), smem=0)
    done_far = over_pair(done)
    dq_far = lax.optimization_barrier((dq_far, near_sum))[0]
    dk_far, dv_near, _ = lax.optimization_barrier((dk_far, dv_near, done))

    dq, dq_near = call(sum_split, [((HD, BLK), BF16)] * 2, (dq, far(dq_far, "x")), smem=0)
    mixed, mixed_near = call(
        sum_split, [((32, 2048), BF16)] * 2, (mixed, far(mixed_far, "y")), smem=0, after=(done,)
    )
    mixed_other = near(mixed_near, "y")
    (stack,) = call(weight_stack, [((2 * HD, BLK), BF16)], (pos, done, done_far), after=(dq_near,))
    stacks = [stack, near(stack, "x"), far(stack, "x"), opposite(stack, "x")]
    dk, dk_near = call(
        sum_split, [((BLK, HD), BF16)] * 2, (dk, far(dk_far, "zh")), smem=0, after=(mixed_other,)
    )
    dv, dv_far = call(
        sum_split, [((BLK, HD), BF16)] * 2, (dv, near(dv_near, "zh")), smem=0
    )
    dq_near = lax.optimization_barrier((dq_near, stacks[1]))[0]
    out_keep, out_send = call(
        gather_grads,
        [((3 * TILE, HD), BF16)] * 2,
        (dk, near(dk_near, "zh"), dv, far(dv_far, "zh"), dq, near(dq_near, "x")),
        smem=0,
    )

    (here,) = call(
        weight_row, [((2 * HD, 1024), BF16)], (pos, *stacks), after=(out_send,)
    )
    out_recv = over_pair(out_send)
    grad_weight, mixed, written = call(
        weight_out,
        [((2 * HD, 2048), F32), ((32, 2048), BF16), ((8, HD), F32)],
        (pos, here, over_core(here), mixed, mixed_other),
        scratch=[
            pltpu.VMEM((2, 2 * HD, 1024), F32),
            pltpu.VMEM((32, 2048), BF16),
            pltpu.SemaphoreType.DMA((3,)),
        ],
        out_space=[pl.ANY, pl.ANY, pltpu.VMEM],
    )
    grad_q, grad_k, grad_v = call(
        join_heads,
        [((TILE, 2 * HD), BF16)] * 3,
        (pos, out_keep, out_recv),
        scratch=[pltpu.VMEM((3, TILE, 2 * HD), BF16), pltpu.SemaphoreType.DMA((3,))],
        out_space=pl.ANY,
        after=(written,),
    )
    return (mixed[None], grad_q[None], grad_k[None], grad_v[None], grad_weight)


def solution(mesh):
    mesh = Mesh(mesh.devices.reshape(4, 4, 2, 4, 2), AXES)
    tokens = ("x", "zh", "par")
    rows = P("core", tokens, "y")
    blocks = P("core", (*tokens, "y"), None)
    weight = P("y", None)
    return jax.shard_map(
        on_device,
        mesh=mesh,
        in_specs=(rows, rows, rows, weight, blocks, P()),
        out_specs=(blocks, rows, rows, rows, weight),
        check_vma=False,
    )
```

```python
import functools
import math

import jax
import jax.numpy as jnp
from jax import lax
from jax.experimental import pallas as pl
from jax.experimental.pallas import tpu as pltpu
from jax.sharding import Mesh
from jax.sharding import PartitionSpec as P

HD = 128
TILE = 128
BLK = 256
SCALE = HD ** (-0.5)
LOG2E = math.log2(math.e)
LOW = -1e30
F32 = jnp.float32
BF16 = jnp.bfloat16
AXES = ("x", "zh", "par", "y", "core")
X, ZH, PAR, Y, CORE = range(5)
ORDER = (0, 1, 3, 2)
NN = (((1,), (0,)), ((), ()))
NT = (((1,), (1,)), ((), ()))


def dot(a, b, dims=NN):
    return lax.dot_general(a, b, dims, preferred_element_type=F32)


class Position:
    def __getitem__(self, n):
        return lax.axis_index(AXES[n])


def call(
    body, outs, ins, flops=0, scratch=(), smem=1, vmem=48, after=(), space=pltpu.VMEM,
    out_space=pltpu.VMEM,
):
    if isinstance(ins[0], Position):
        place, placed = ins[0], body
        ins, smem = ins[1:], smem - 1

        def body(*refs):
            placed(place, *refs)

    specs = [pl.BlockSpec(memory_space=pltpu.SMEM)] * smem
    specs += [pl.BlockSpec(memory_space=space)] * (len(ins) - smem)
    used = len(ins)
    out_spaces = out_space if isinstance(out_space, list) else [out_space] * len(outs)
    if after:
        specs += [pl.BlockSpec(memory_space=pl.ANY)] * len(after)
        inner = body

        def body(*refs):
            inner(*refs[:used], *refs[used + len(after) :])

    shapes = [jax.ShapeDtypeStruct(s, d) for s, d in outs]
    moved = sum(math.prod(a.shape) * a.dtype.itemsize for a in list(ins) + shapes)
    ins = tuple(ins) + tuple(after)
    return pl.pallas_call(
        body,
        out_shape=shapes,
        in_specs=specs,
        out_specs=[pl.BlockSpec(memory_space=place) for place in out_spaces],
        scratch_shapes=list(scratch),
        compiler_params=pltpu.CompilerParams(vmem_limit_bytes=vmem * 2**20),
        cost_estimate=pl.CostEstimate(flops=flops, bytes_accessed=moved, transcendentals=0),
    )(*ins)


def own_blocks(keep, recv, k, v, q):
    for n, ref in ((0, q), (1, k), (2, v)):
        rows = slice(n * TILE, (n + 1) * TILE)
        ref[:TILE, :] = keep[rows, :]
        ref[TILE:, :] = recv[rows, :]


def copy_rows(rows, out):
    out[...] = rows[...]


def stack_two(a, b, out):
    rows = a.shape[0]
    out[:rows, :] = a[...]
    out[rows:, :] = b[...]


def stack_pairs(k0, k1, v0, v1, q0, q1, k, v, q):
    stack_two(k0, k1, k)
    stack_two(v0, v1, v)
    stack_two(q0, q1, q)


def join_rows(pos, pair, other, near, far):
    for n in range(4):
        ref = (pair, other)[n // 2]
        start = (n % 2) * 64
        rows = pl.ds(pl.multiple_of((pos[Y] ^ ORDER[n]) * 32, 32), 32)
        near[rows, :] = ref[start : start + 32, :]
        far[rows, :] = ref[start + 32 : start + 64, :]


def bias_rows(pos, mask, query_x):
    lane = lax.broadcasted_iota(jnp.int32, (1, BLK), 1)
    par = pos[PAR]
    query = (query_x * 4 + pos[ZH]) * 2
    rows = []
    for e in ORDER:
        key = (pos[X] * 4 + (pos[ZH] ^ e)) * 2
        for tile in (par, 1 - par):
            near = jnp.where(mask[query + par, key + tile] > 0, 0.0, LOW)
            far = jnp.where(mask[query + 1 - par, key + tile] > 0, 0.0, LOW)
            rows.append(jnp.where(lane < TILE, near, far))
    return rows


def scores_of(keys, queries, rows):
    raw = dot(keys, queries, NT) * (SCALE * LOG2E)
    return jnp.concatenate(
        [raw[t * TILE : (t + 1) * TILE] + row for t, row in enumerate(rows)], axis=0
    )


def split3(value):
    high = value.astype(BF16).astype(F32)
    rest = value - high
    middle = rest.astype(BF16).astype(F32)
    low = (rest - middle).astype(BF16).astype(F32)
    return high, middle, low


def pack_rows(values):
    row = lax.broadcasted_iota(jnp.int32, (16, BLK), 0)
    packed = jnp.zeros((16, BLK), F32)
    for n, value in enumerate(values):
        packed = jnp.where(row == n, value, packed)
    return packed.astype(BF16)


def load_kv(kp, kf, vp, vn):
    keys = jnp.concatenate([kp[...], kf[...]], axis=0)
    values = [vp[:BLK, :], vn[:BLK, :], vp[BLK:, :], vn[BLK:, :]]
    return keys, jnp.concatenate(values, axis=0)


def transposed(a):
    return a.astype(F32).T.astype(BF16)


def query_block(qp, qf, n):
    return (qp, qf)[n // 2][(n % 2) * BLK : (n % 2 + 1) * BLK, :]


def forward(pos, mask, kp, kf, vp, vn, qp, qf, p0, p1, p2, p3):
    keys, values = load_kv(kp, kf, vp, vn)
    values_t = transposed(values)
    for n, pack in enumerate((p0, p1, p2, p3)):
        rows = bias_rows(pos, mask, pos[X] ^ ORDER[n])
        queries = query_block(qp, qf, n)
        scores = [
            scores_of(keys[e * BLK : (e + 1) * BLK], queries, rows[2 * e : 2 * e + 2])
            for e in range(4)
        ]
        largest = functools.reduce(
            jnp.maximum, [jnp.max(block, axis=0, keepdims=True) for block in scores]
        )
        largest = jnp.maximum(largest, 0.1 * LOW)
        total = jnp.zeros((1, BLK), F32)
        summed = jnp.zeros((HD, BLK), F32)
        for e in range(4):
            weights = jnp.exp2(scores[e] - largest)
            total = total + jnp.sum(weights, axis=0, keepdims=True)
            summed = summed + dot(values_t[:, e * BLK : (e + 1) * BLK], weights.astype(BF16))
        some = total > 0.0
        safe = jnp.where(some, total, 1.0)
        pack[:HD, :] = (summed / safe).astype(BF16)
        pack[HD:, :] = pack_rows(split3(jnp.where(some, largest + jnp.log2(safe), LOW)))


def backward(
    pos, mask, kp, kf, vp, vn, qp, qf, s0, s1, s2, s3,
    dk, dk_far, dv, dv_near, dq, dq_far, probs_of, scores_grad_of,
):
    keys, values = load_kv(kp, kf, vp, vn)
    keys_t = transposed(keys)
    for n, ref in enumerate((s0, s1, s2, s3)):
        rows = bias_rows(pos, mask, pos[X] ^ ORDER[n])
        s = ref[2 * HD :, :].astype(F32)
        lse = s[0:1] + s[1:2] + s[2:3]
        delta = s[3:4] + s[4:5] + s[5:6]
        probs = jnp.exp2(scores_of(keys, query_block(qp, qf, n), rows) - lse)
        grad_probs = dot(values, ref[HD : 2 * HD, :])
        grad_scores = (probs * (grad_probs - delta)).astype(BF16)
        columns = slice(n * BLK, (n + 1) * BLK)
        probs_of[:, columns] = probs.astype(BF16)
        scores_grad_of[:, columns] = grad_scores
        out = (dq, dq_far)[n // 2]
        out[(n % 2) * HD : (n % 2 + 1) * HD, :] = (dot(keys_t, grad_scores) * SCALE).astype(BF16)
    queries = jnp.concatenate([qp[...], qf[...]], axis=0)
    grads = jnp.concatenate([ref[HD : 2 * HD, :] for ref in (s0, s1, s2, s3)], axis=1)
    for n in range(4):
        block = slice(n * BLK, (n + 1) * BLK)
        half = slice((n % 2) * BLK, (n % 2 + 1) * BLK)
        out = (dk, dk_far)[n // 2]
        out[half, :] = (dot(scores_grad_of[block, :], queries) * SCALE).astype(BF16)
        half = slice((n // 2) * BLK, (n // 2 + 1) * BLK)
        out = (dv, dv_near)[n % 2]
        out[half, :] = dot(probs_of[block, :], grads, NT).astype(BF16)


def back_project(pos, w, near, far, grads):
    head = w[pl.ds(pl.multiple_of(pos[PAR] * HD, HD), HD), :]
    grads[:, :TILE] = dot(head, near[...], NT).astype(BF16)
    grads[:, TILE:] = dot(head, far[...], NT).astype(BF16)


def attend(pos, p0, p1, p2, p3, grads, near, far, att, stats, keep, send):
    lses, parts = [], []
    for pack in (p0, p1, p2, p3):
        parts.append(pack[:HD, :].astype(F32))
        s = pack[HD:, :].astype(F32)
        lses.append(s[0:1] + s[1:2] + s[2:3])
    largest = functools.reduce(jnp.maximum, lses)
    weights = [jnp.exp2(v - largest) for v in lses]
    total = sum(weights)
    out = sum((w / total) * p for w, p in zip(weights, parts)).astype(BF16)
    att[...] = out
    delta = jnp.sum(grads[...].astype(F32) * out.astype(F32), axis=0, keepdims=True)
    stats[...] = pack_rows(split3(largest + jnp.log2(total)) + split3(delta))
    both = dot(out[:, :TILE], near[...]) + dot(out[:, TILE:], far[...])

    @pl.when(pos[CORE] == 0)
    def _():
        keep[...] = both[:, :1024]
        send[...] = both[:, 1024:].astype(BF16)

    @pl.when(pos[CORE] != 0)
    def _():
        keep[...] = both[:, 1024:]
        send[...] = both[:, :1024].astype(BF16)


def weight_cut(pos, mine, other, grads, stats, b0, b1, b2, b3):
    for n, ref in enumerate((b0, b1, b2, b3)):
        columns = pl.ds(pl.multiple_of((pos[X] ^ ORDER[n]) * BLK, BLK), BLK)
        ref[:HD, :] = (mine[:, columns] + other[:, columns].astype(F32)).astype(BF16)
        ref[HD : 2 * HD, :] = grads[...]
        ref[2 * HD :, :] = stats[...]


def add(a, b):
    return a.astype(F32) + b.astype(F32)


def sum_cuts(a, b, c, d, out):
    out[...] = (add(a[:HD, :], b[:HD, :]) + add(c[:HD, :], d[:HD, :])).astype(BF16)


def sum_two(a, b, out):
    out[...] = add(a[...], b[...]).astype(BF16)


def sum_split(a, b, keep, send):
    total = add(a[...], b[...]).astype(BF16)
    rows = keep.shape[0]
    keep[...] = total[:rows]
    send[...] = total[rows:]


def weight_stack(pos, mine, other, out):
    out[pl.ds(pl.multiple_of(pos[PAR] * HD, HD), HD), :] = mine[...]
    out[pl.ds(pl.multiple_of((1 - pos[PAR]) * HD, HD), HD), :] = other[...]


def weight_row(pos, f0, f1, f2, f3, out):
    for n, ref in enumerate((f0, f1, f2, f3)):
        columns = pl.ds(pl.multiple_of((pos[X] ^ ORDER[n]) * BLK, BLK), BLK)
        out[:, columns] = ref[...]


def mix(pos, att, other, w, out, out_far, full):
    mine_rows = pl.ds(pl.multiple_of(pos[PAR] * HD, HD), HD)
    other_rows = pl.ds(pl.multiple_of((1 - pos[PAR]) * HD, HD), HD)
    mine_t = att[:, :TILE].astype(F32).T.astype(BF16)
    other_t = other[...].astype(F32).T.astype(BF16)
    full[...] = (dot(mine_t, w[mine_rows, :]) + dot(other_t, w[other_rows, :])).astype(BF16)
    for n in range(4):
        rows = pl.ds(pl.multiple_of((pos[Y] ^ ORDER[n]) * 32, 32), 32)
        (out, out_far)[n // 2][(n % 2) * 32 : (n % 2 + 1) * 32, :] = full[rows, :]


def gather_grads(k, k_near, v, v_far, q, q_near, keep, send):
    q = add(q[...], q_near[...])
    keep[:TILE, :] = q[:, :TILE].T.astype(BF16)
    send[:TILE, :] = q[:, TILE:].T.astype(BF16)
    for n, (mine, other) in enumerate(((k, k_near), (v, v_far))):
        total = add(mine[...], other[...]).astype(BF16)
        rows = slice((n + 1) * TILE, (n + 2) * TILE)
        keep[rows, :] = total[:TILE]
        send[rows, :] = total[TILE:]


def weight_out(pos, here, core, mix_mine, mix_other, weight, mixed, flag, halves, rows_out, sems):
    copies = []
    flag[...] = jnp.zeros_like(flag)
    for n, (half, ref) in enumerate(((pos[CORE], here), (1 - pos[CORE], core))):
        halves[n] = ref[...].astype(F32)
        columns = pl.ds(pl.multiple_of(half * 1024, 1024), 1024)
        copies.append(pltpu.make_async_copy(halves.at[n], weight.at[:, columns], sems.at[n]))
        copies[-1].start()
    rows_out[...] = add(mix_mine[...], mix_other[...]).astype(BF16)
    copies.append(pltpu.make_async_copy(rows_out, mixed, sems.at[2]))
    copies[-1].start()
    for copy in copies:
        copy.wait()


def join_heads(pos, mine, other, q, k, v, heads, sems):
    left = pl.ds(pl.multiple_of(pos[PAR] * HD, HD), HD)
    right = pl.ds(pl.multiple_of((1 - pos[PAR]) * HD, HD), HD)
    copies = []
    for n, ref in enumerate((q, k, v)):
        rows = slice(n * TILE, (n + 1) * TILE)
        heads[n, :, left] = mine[rows, :]
        heads[n, :, right] = other[rows, :]
        copies.append(pltpu.make_async_copy(heads.at[n], ref, sems.at[n]))
        copies[-1].start()
    for copy in copies:
        copy.wait()


def near(a, axis):
    return lax.ppermute(a, axis, [(0, 1), (1, 0), (2, 3), (3, 2)])


def far(a, axis):
    return lax.ppermute(a, axis, [(0, 3), (3, 0), (1, 2), (2, 1)])


def opposite(a, axis):
    return lax.ppermute(a, axis, [(0, 2), (2, 0), (1, 3), (3, 1)])


def over_pair(a):
    return lax.ppermute(a, "par", [(0, 1), (1, 0)])


def over_core(a):
    return lax.ppermute(a, "core", [(0, 1), (1, 0)])


def on_device(query_rows, key_rows, value_rows, out_weight, cotangent, tile_mask):
    pos = Position()
    kv_mm = 2 * 1024 * 1024 * HD

    inputs = (query_rows[0], key_rows[0], value_rows[0])
    first = pos[PAR] == 0
    send = jnp.concatenate([jnp.where(first, rows[:, HD:], rows[:, :HD]) for rows in inputs])
    keep = jnp.concatenate([jnp.where(first, rows[:, :HD], rows[:, HD:]) for rows in inputs])
    recv = over_pair(send)
    rows_far = over_pair(cotangent[0])
    (rows,) = call(copy_rows, [((32, 2048), BF16)], (cotangent[0],), smem=0, after=(send,))
    k, v, q = call(own_blocks, [((BLK, HD), BF16)] * 3, (keep, recv), smem=0)
    (rows,) = call(stack_two, [((64, 2048), BF16)], (rows, rows_far), smem=0, after=(recv,))
    kp, vp, qp = call(
        stack_pairs,
        [((2 * BLK, HD), BF16)] * 3,
        (k, near(k, "zh"), v, far(v, "zh"), q, near(q, "x")),
        smem=0,
    )
    (rows,) = call(stack_two, [((TILE, 2048), BF16)], (rows, near(rows, "y")), smem=0, after=(kp,))
    kf, vn, qf, rows_far = far(kp, "zh"), near(vp, "zh"), far(qp, "x"), far(rows, "y")

    packs = call(
        forward,
        [((HD + 16, BLK), BF16)] * 4,
        (pos, tile_mask, kp, kf, vp, vn, qp, qf),
        flops=2 * kv_mm,
        smem=2,
    )
    packs = [packs[0], near(packs[1], "x"), far(packs[2], "x"), opposite(packs[3], "x")]

    cot, cot_far = call(join_rows, [((TILE, 2048), BF16)] * 2, (pos, rows, rows_far))
    (grads,) = call(
        back_project,
        [((HD, BLK), BF16)],
        (pos, out_weight, cot, cot_far),
        flops=2 * HD * BLK * 2048,
    )
    att, stats, gw_keep, gw_send = call(
        attend,
        [((HD, BLK), BF16), ((16, BLK), BF16), ((HD, 1024), F32), ((HD, 1024), BF16)],
        (pos, *packs, grads, cot, cot_far),
        flops=2 * HD * BLK * 2048,
    )
    gw_recv = over_core(gw_send)
    cuts = call(
        weight_cut, [((2 * HD + 16, BLK), BF16)] * 4, (pos, gw_keep, gw_recv, grads, stats)
    )
    cuts = [cuts[0], near(cuts[1], "x"), far(cuts[2], "x"), opposite(cuts[3], "x")]
    att_far = over_pair(att[:, TILE:])
    mixed, mixed_far = call(
        mix,
        [((64, 2048), BF16)] * 2,
        (pos, att, att_far, out_weight),
        flops=2 * TILE * 256 * 2048,
        scratch=[pltpu.VMEM((TILE, 2048), BF16)],
    )
    (share,) = call(sum_cuts, [((HD, BLK), BF16)], cuts, smem=0, after=(mixed_far,))

    dk, dk_far, dv, dv_near, dq, dq_far = call(
        backward,
        [((2 * BLK, HD), BF16)] * 4 + [((2 * HD, BLK), BF16)] * 2,
        (pos, tile_mask, kp, kf, vp, vn, qp, qf, *cuts),
        flops=5 * kv_mm,
        scratch=[pltpu.VMEM((4 * BLK, 4 * BLK), BF16)] * 2,
        smem=2,
        after=(share,),
    )
    (near_sum,) = call(
        sum_two, [((HD, BLK), BF16)], (share, near(share, "zh")), smem=0, after=(dq,)
    )
    (done,) = call(sum_two, [((HD, BLK), BF16)], (near_sum, far(near_sum, "zh")), smem=0)
    done_far = over_pair(done)
    dq_far = lax.optimization_barrier((dq_far, near_sum))[0]
    dk_far, dv_near, _ = lax.optimization_barrier((dk_far, dv_near, done))

    dq, dq_near = call(sum_split, [((HD, BLK), BF16)] * 2, (dq, far(dq_far, "x")), smem=0)
    mixed, mixed_near = call(
        sum_split, [((32, 2048), BF16)] * 2, (mixed, far(mixed_far, "y")), smem=0, after=(done,)
    )
    mixed_other = near(mixed_near, "y")
    (stack,) = call(weight_stack, [((2 * HD, BLK), BF16)], (pos, done, done_far), after=(dq_near,))
    stacks = [stack, near(stack, "x"), far(stack, "x"), opposite(stack, "x")]
    dk, dk_near = call(
        sum_split, [((BLK, HD), BF16)] * 2, (dk, far(dk_far, "zh")), smem=0, after=(mixed_other,)
    )
    dv, dv_far = call(
        sum_split, [((BLK, HD), BF16)] * 2, (dv, near(dv_near, "zh")), smem=0
    )
    dq_near = lax.optimization_barrier((dq_near, stacks[1]))[0]
    out_keep, out_send = call(
        gather_grads,
        [((3 * TILE, HD), BF16)] * 2,
        (dk, near(dk_near, "zh"), dv, far(dv_far, "zh"), dq, near(dq_near, "x")),
        smem=0,
    )

    (here,) = call(
        weight_row, [((2 * HD, 1024), BF16)], (pos, *stacks), after=(out_send,)
    )
    out_recv = over_pair(out_send)
    grad_weight, mixed, written = call(
        weight_out,
        [((2 * HD, 2048), F32), ((32, 2048), BF16), ((8, HD), F32)],
        (pos, here, over_core(here), mixed, mixed_other),
        scratch=[
            pltpu.VMEM((2, 2 * HD, 1024), F32),
            pltpu.VMEM((32, 2048), BF16),
            pltpu.SemaphoreType.DMA((3,)),
        ],
        out_space=[pl.ANY, pl.ANY, pltpu.VMEM],
    )
    grad_q, grad_k, grad_v = call(
        join_heads,
        [((TILE, 2 * HD), BF16)] * 3,
        (pos, out_keep, out_recv),
        scratch=[pltpu.VMEM((3, TILE, 2 * HD), BF16), pltpu.SemaphoreType.DMA((3,))],
        out_space=pl.ANY,
        after=(written,),
    )
    return (mixed[None], grad_q[None], grad_k[None], grad_v[None], grad_weight)


def solution(mesh):
    mesh = Mesh(mesh.devices.reshape(4, 4, 2, 4, 2), AXES)
    tokens = ("x", "zh", "par")
    rows = P("core", tokens, "y")
    blocks = P("core", (*tokens, "y"), None)
    weight = P("y", None)
    return jax.shard_map(
        on_device,
        mesh=mesh,
        in_specs=(rows, rows, rows, weight, blocks, P()),
        out_specs=(blocks, rows, rows, rows, weight),
        check_vma=False,
    )
```

```python
import functools
import math

import jax
import jax.numpy as jnp
from jax import lax
from jax.experimental import pallas as pl
from jax.experimental.pallas import tpu as pltpu
from jax.sharding import Mesh
from jax.sharding import PartitionSpec as P

HD = 128
TILE = 128
BLK = 256
SCALE = HD ** (-0.5)
LOG2E = math.log2(math.e)
LOW = -1e30
F32 = jnp.float32
BF16 = jnp.bfloat16
AXES = ("x", "zh", "par", "y", "core")
X, ZH, PAR, Y, CORE = range(5)
ORDER = (0, 1, 3, 2)
NN = (((1,), (0,)), ((), ()))
NT = (((1,), (1,)), ((), ()))


def dot(a, b, dims=NN):
    return lax.dot_general(a, b, dims, preferred_element_type=F32)


class Position:
    def __getitem__(self, n):
        return lax.axis_index(AXES[n])


def call(
    body, outs, ins, flops=0, scratch=(), smem=1, vmem=48, after=(), space=pltpu.VMEM,
    out_space=pltpu.VMEM,
):
    if isinstance(ins[0], Position):
        place, placed = ins[0], body
        ins, smem = ins[1:], smem - 1

        def body(*refs):
            placed(place, *refs)

    specs = [pl.BlockSpec(memory_space=pltpu.SMEM)] * smem
    specs += [pl.BlockSpec(memory_space=space)] * (len(ins) - smem)
    used = len(ins)
    out_spaces = out_space if isinstance(out_space, list) else [out_space] * len(outs)
    if after:
        specs += [pl.BlockSpec(memory_space=pl.ANY)] * len(after)
        inner = body

        def body(*refs):
            inner(*refs[:used], *refs[used + len(after) :])

    shapes = [jax.ShapeDtypeStruct(s, d) for s, d in outs]
    moved = sum(math.prod(a.shape) * a.dtype.itemsize for a in list(ins) + shapes)
    ins = tuple(ins) + tuple(after)
    return pl.pallas_call(
        body,
        out_shape=shapes,
        in_specs=specs,
        out_specs=[pl.BlockSpec(memory_space=place) for place in out_spaces],
        scratch_shapes=list(scratch),
        compiler_params=pltpu.CompilerParams(vmem_limit_bytes=vmem * 2**20),
        cost_estimate=pl.CostEstimate(flops=flops, bytes_accessed=moved, transcendentals=0),
    )(*ins)


def own_blocks(keep, recv, k, v, q):
    for n, ref in ((0, q), (1, k), (2, v)):
        rows = slice(n * TILE, (n + 1) * TILE)
        ref[:TILE, :] = keep[rows, :]
        ref[TILE:, :] = recv[rows, :]


def early_rows(pos, mask, rows, out, bias):
    out[...] = rows[...]
    for n in range(4):
        for t, row in enumerate(bias_rows(pos, mask, pos[X] ^ ORDER[n])):
            bias[n * 8 + t : n * 8 + t + 1, :] = row


def stack_two(a, b, out):
    rows = a.shape[0]
    out[:rows, :] = a[...]
    out[rows:, :] = b[...]


def stack_pairs(k0, k1, v0, v1, q0, q1, k, v, q):
    stack_two(k0, k1, k)
    stack_two(v0, v1, v)
    stack_two(q0, q1, q)


def join_rows(pos, pair, other, near, far):
    for n in range(4):
        ref = (pair, other)[n // 2]
        start = (n % 2) * 64
        rows = pl.ds(pl.multiple_of((pos[Y] ^ ORDER[n]) * 32, 32), 32)
        near[rows, :] = ref[start : start + 32, :]
        far[rows, :] = ref[start + 32 : start + 64, :]


def bias_rows(pos, mask, query_x):
    lane = lax.broadcasted_iota(jnp.int32, (1, BLK), 1)
    par = pos[PAR]
    query = (query_x * 4 + pos[ZH]) * 2
    rows = []
    for e in ORDER:
        key = (pos[X] * 4 + (pos[ZH] ^ e)) * 2
        for tile in (par, 1 - par):
            near = jnp.where(mask[query + par, key + tile] > 0, 0.0, LOW)
            far = jnp.where(mask[query + 1 - par, key + tile] > 0, 0.0, LOW)
            rows.append(jnp.where(lane < TILE, near, far))
    return rows


def scores_of(keys, queries, rows):
    raw = dot(keys, queries, NT) * (SCALE * LOG2E)
    return jnp.concatenate(
        [raw[t * TILE : (t + 1) * TILE] + row for t, row in enumerate(rows)], axis=0
    )


def split3(value):
    high = value.astype(BF16).astype(F32)
    rest = value - high
    middle = rest.astype(BF16).astype(F32)
    low = (rest - middle).astype(BF16).astype(F32)
    return high, middle, low


def pack_rows(values):
    row = lax.broadcasted_iota(jnp.int32, (16, BLK), 0)
    packed = jnp.zeros((16, BLK), F32)
    for n, value in enumerate(values):
        packed = jnp.where(row == n, value, packed)
    return packed.astype(BF16)


def load_kv(kp, kf, vp, vn):
    keys = jnp.concatenate([kp[...], kf[...]], axis=0)
    values = [vp[:BLK, :], vn[:BLK, :], vp[BLK:, :], vn[BLK:, :]]
    return keys, jnp.concatenate(values, axis=0)


def transposed(a):
    return a.astype(F32).T.astype(BF16)


def query_block(qp, qf, n):
    return (qp, qf)[n // 2][(n % 2) * BLK : (n % 2 + 1) * BLK, :]


def forward(bias, kp, kf, vp, vn, qp, qf, p0, p1, p2, p3):
    keys, values = load_kv(kp, kf, vp, vn)
    values_t = transposed(values)
    for n, pack in enumerate((p0, p1, p2, p3)):
        rows = [bias[n * 8 + t : n * 8 + t + 1, :] for t in range(8)]
        queries = query_block(qp, qf, n)
        scores = [
            scores_of(keys[e * BLK : (e + 1) * BLK], queries, rows[2 * e : 2 * e + 2])
            for e in range(4)
        ]
        largest = functools.reduce(
            jnp.maximum, [jnp.max(block, axis=0, keepdims=True) for block in scores]
        )
        largest = jnp.maximum(largest, 0.1 * LOW)
        total = jnp.zeros((1, BLK), F32)
        summed = jnp.zeros((HD, BLK), F32)
        for e in range(4):
            weights = jnp.exp2(scores[e] - largest)
            total = total + jnp.sum(weights, axis=0, keepdims=True)
            summed = summed + dot(values_t[:, e * BLK : (e + 1) * BLK], weights.astype(BF16))
        some = total > 0.0
        safe = jnp.where(some, total, 1.0)
        pack[:HD, :] = (summed / safe).astype(BF16)
        pack[HD:, :] = pack_rows(split3(jnp.where(some, largest + jnp.log2(safe), LOW)))


def backward(
    bias, kp, kf, vp, vn, qp, qf, s0, s1, s2, s3,
    dk, dk_far, dv, dv_near, dq, dq_far, probs_of, scores_grad_of,
):
    keys, values = load_kv(kp, kf, vp, vn)
    keys_t = transposed(keys)
    for n, ref in enumerate((s0, s1, s2, s3)):
        rows = [bias[n * 8 + t : n * 8 + t + 1, :] for t in range(8)]
        s = ref[2 * HD :, :].astype(F32)
        lse = s[0:1] + s[1:2] + s[2:3]
        delta = s[3:4] + s[4:5] + s[5:6]
        probs = jnp.exp2(scores_of(keys, query_block(qp, qf, n), rows) - lse)
        grad_probs = dot(values, ref[HD : 2 * HD, :])
        grad_scores = (probs * (grad_probs - delta)).astype(BF16)
        columns = slice(n * BLK, (n + 1) * BLK)
        probs_of[:, columns] = probs.astype(BF16)
        scores_grad_of[:, columns] = grad_scores
        out = (dq, dq_far)[n // 2]
        out[(n % 2) * HD : (n % 2 + 1) * HD, :] = (dot(keys_t, grad_scores) * SCALE).astype(BF16)
    queries = jnp.concatenate([qp[...], qf[...]], axis=0)
    grads = jnp.concatenate([ref[HD : 2 * HD, :] for ref in (s0, s1, s2, s3)], axis=1)
    for n in range(4):
        block = slice(n * BLK, (n + 1) * BLK)
        half = slice((n % 2) * BLK, (n % 2 + 1) * BLK)
        out = (dk, dk_far)[n // 2]
        out[half, :] = (dot(scores_grad_of[block, :], queries) * SCALE).astype(BF16)
        half = slice((n // 2) * BLK, (n // 2 + 1) * BLK)
        out = (dv, dv_near)[n % 2]
        out[half, :] = dot(probs_of[block, :], grads, NT).astype(BF16)


def back_project(pos, w, near, far, grads):
    head = w[pl.ds(pl.multiple_of(pos[PAR] * HD, HD), HD), :]
    grads[:, :TILE] = dot(head, near[...], NT).astype(BF16)
    grads[:, TILE:] = dot(head, far[...], NT).astype(BF16)


def attend(pos, p0, p1, p2, p3, grads, near, far, att, stats, keep, send):
    lses, parts = [], []
    for pack in (p0, p1, p2, p3):
        parts.append(pack[:HD, :].astype(F32))
        s = pack[HD:, :].astype(F32)
        lses.append(s[0:1] + s[1:2] + s[2:3])
    largest = functools.reduce(jnp.maximum, lses)
    weights = [jnp.exp2(v - largest) for v in lses]
    total = sum(weights)
    out = sum((w / total) * p for w, p in zip(weights, parts)).astype(BF16)
    att[...] = out
    delta = jnp.sum(grads[...].astype(F32) * out.astype(F32), axis=0, keepdims=True)
    stats[...] = pack_rows(split3(largest + jnp.log2(total)) + split3(delta))
    both = dot(out[:, :TILE], near[...]) + dot(out[:, TILE:], far[...])

    @pl.when(pos[CORE] == 0)
    def _():
        keep[...] = both[:, :1024]
        send[...] = both[:, 1024:].astype(BF16)

    @pl.when(pos[CORE] != 0)
    def _():
        keep[...] = both[:, 1024:]
        send[...] = both[:, :1024].astype(BF16)


def weight_cut(pos, mine, other, grads, stats, b0, b1, b2, b3):
    for n, ref in enumerate((b0, b1, b2, b3)):
        columns = pl.ds(pl.multiple_of((pos[X] ^ ORDER[n]) * BLK, BLK), BLK)
        ref[:HD, :] = (mine[:, columns] + other[:, columns].astype(F32)).astype(BF16)
        ref[HD : 2 * HD, :] = grads[...]
        ref[2 * HD :, :] = stats[...]


def add(a, b):
    return a.astype(F32) + b.astype(F32)


def sum_cuts(a, b, c, d, out):
    out[...] = (add(a[:HD, :], b[:HD, :]) + add(c[:HD, :], d[:HD, :])).astype(BF16)


def sum_two(a, b, out):
    out[...] = add(a[...], b[...]).astype(BF16)


def sum_split(a, b, keep, send):
    total = add(a[...], b[...]).astype(BF16)
    rows = keep.shape[0]
    keep[...] = total[:rows]
    send[...] = total[rows:]


def weight_stack(pos, mine, other, out):
    out[pl.ds(pl.multiple_of(pos[PAR] * HD, HD), HD), :] = mine[...]
    out[pl.ds(pl.multiple_of((1 - pos[PAR]) * HD, HD), HD), :] = other[...]


def weight_row(pos, f0, f1, f2, f3, out):
    for n, ref in enumerate((f0, f1, f2, f3)):
        columns = pl.ds(pl.multiple_of((pos[X] ^ ORDER[n]) * BLK, BLK), BLK)
        out[:, columns] = ref[...]


def mix(pos, att, other, w, out, out_far, full):
    mine_rows = pl.ds(pl.multiple_of(pos[PAR] * HD, HD), HD)
    other_rows = pl.ds(pl.multiple_of((1 - pos[PAR]) * HD, HD), HD)
    mine_t = att[:, :TILE].astype(F32).T.astype(BF16)
    other_t = other[...].astype(F32).T.astype(BF16)
    full[...] = (dot(mine_t, w[mine_rows, :]) + dot(other_t, w[other_rows, :])).astype(BF16)
    for n in range(4):
        rows = pl.ds(pl.multiple_of((pos[Y] ^ ORDER[n]) * 32, 32), 32)
        (out, out_far)[n // 2][(n % 2) * 32 : (n % 2 + 1) * 32, :] = full[rows, :]


def gather_grads(k, k_near, v, v_far, q, q_near, keep, send):
    q = add(q[...], q_near[...])
    keep[:TILE, :] = q[:, :TILE].T.astype(BF16)
    send[:TILE, :] = q[:, TILE:].T.astype(BF16)
    for n, (mine, other) in enumerate(((k, k_near), (v, v_far))):
        total = add(mine[...], other[...]).astype(BF16)
        rows = slice((n + 1) * TILE, (n + 2) * TILE)
        keep[rows, :] = total[:TILE]
        send[rows, :] = total[TILE:]


def weight_out(pos, here, core, mix_mine, mix_other, weight, mixed, flag, halves, rows_out, sems):
    copies = []
    flag[...] = jnp.zeros_like(flag)
    for n, (half, ref) in enumerate(((pos[CORE], here), (1 - pos[CORE], core))):
        halves[n] = ref[...].astype(F32)
        columns = pl.ds(pl.multiple_of(half * 1024, 1024), 1024)
        copies.append(pltpu.make_async_copy(halves.at[n], weight.at[:, columns], sems.at[n]))
        copies[-1].start()
    rows_out[...] = add(mix_mine[...], mix_other[...]).astype(BF16)
    copies.append(pltpu.make_async_copy(rows_out, mixed, sems.at[2]))
    copies[-1].start()
    for copy in copies:
        copy.wait()


def join_heads(pos, mine, other, q, k, v, heads, sems):
    left = pl.ds(pl.multiple_of(pos[PAR] * HD, HD), HD)
    right = pl.ds(pl.multiple_of((1 - pos[PAR]) * HD, HD), HD)
    copies = []
    for n, ref in enumerate((q, k, v)):
        rows = slice(n * TILE, (n + 1) * TILE)
        heads[n, :, left] = mine[rows, :]
        heads[n, :, right] = other[rows, :]
        copies.append(pltpu.make_async_copy(heads.at[n], ref, sems.at[n]))
        copies[-1].start()
    for copy in copies:
        copy.wait()


def near(a, axis):
    return lax.ppermute(a, axis, [(0, 1), (1, 0), (2, 3), (3, 2)])


def far(a, axis):
    return lax.ppermute(a, axis, [(0, 3), (3, 0), (1, 2), (2, 1)])


def opposite(a, axis):
    return lax.ppermute(a, axis, [(0, 2), (2, 0), (1, 3), (3, 1)])


def over_pair(a):
    return lax.ppermute(a, "par", [(0, 1), (1, 0)])


def over_core(a):
    return lax.ppermute(a, "core", [(0, 1), (1, 0)])


def on_device(query_rows, key_rows, value_rows, out_weight, cotangent, tile_mask):
    pos = Position()
    kv_mm = 2 * 1024 * 1024 * HD

    inputs = (query_rows[0], key_rows[0], value_rows[0])
    first = pos[PAR] == 0
    send = jnp.concatenate([jnp.where(first, rows[:, HD:], rows[:, :HD]) for rows in inputs])
    keep = jnp.concatenate([jnp.where(first, rows[:, :HD], rows[:, HD:]) for rows in inputs])
    recv = over_pair(send)
    rows_far = over_pair(cotangent[0])
    rows, bias = call(
        early_rows,
        [((32, 2048), BF16), ((32, BLK), F32)],
        (pos, tile_mask, cotangent[0]),
        smem=2,
        after=(send,),
    )
    k, v, q = call(own_blocks, [((BLK, HD), BF16)] * 3, (keep, recv), smem=0)
    (rows,) = call(stack_two, [((64, 2048), BF16)], (rows, rows_far), smem=0, after=(recv,))
    kp, vp, qp = call(
        stack_pairs,
        [((2 * BLK, HD), BF16)] * 3,
        (k, near(k, "zh"), v, far(v, "zh"), q, near(q, "x")),
        smem=0,
    )
    (rows,) = call(stack_two, [((TILE, 2048), BF16)], (rows, near(rows, "y")), smem=0, after=(kp,))
    kf, vn, qf, rows_far = far(kp, "zh"), near(vp, "zh"), far(qp, "x"), far(rows, "y")

    packs = call(
        forward,
        [((HD + 16, BLK), BF16)] * 4,
        (bias, kp, kf, vp, vn, qp, qf),
        flops=2 * kv_mm,
        smem=0,
    )
    packs = [packs[0], near(packs[1], "x"), far(packs[2], "x"), opposite(packs[3], "x")]

    cot, cot_far = call(join_rows, [((TILE, 2048), BF16)] * 2, (pos, rows, rows_far))
    (grads,) = call(
        back_project,
        [((HD, BLK), BF16)],
        (pos, out_weight, cot, cot_far),
        flops=2 * HD * BLK * 2048,
    )
    att, stats, gw_keep, gw_send = call(
        attend,
        [((HD, BLK), BF16), ((16, BLK), BF16), ((HD, 1024), F32), ((HD, 1024), BF16)],
        (pos, *packs, grads, cot, cot_far),
        flops=2 * HD * BLK * 2048,
    )
    gw_recv = over_core(gw_send)
    cuts = call(
        weight_cut, [((2 * HD + 16, BLK), BF16)] * 4, (pos, gw_keep, gw_recv, grads, stats)
    )
    cuts = [cuts[0], near(cuts[1], "x"), far(cuts[2], "x"), opposite(cuts[3], "x")]
    att_far = over_pair(att[:, TILE:])
    mixed, mixed_far = call(
        mix,
        [((64, 2048), BF16)] * 2,
        (pos, att, att_far, out_weight),
        flops=2 * TILE * 256 * 2048,
        scratch=[pltpu.VMEM((TILE, 2048), BF16)],
    )
    (share,) = call(sum_cuts, [((HD, BLK), BF16)], cuts, smem=0, after=(mixed_far,))

    dk, dk_far, dv, dv_near, dq, dq_far = call(
        backward,
        [((2 * BLK, HD), BF16)] * 4 + [((2 * HD, BLK), BF16)] * 2,
        (bias, kp, kf, vp, vn, qp, qf, *cuts),
        flops=5 * kv_mm,
        scratch=[pltpu.VMEM((4 * BLK, 4 * BLK), BF16)] * 2,
        smem=0,
        after=(share,),
    )
    (near_sum,) = call(
        sum_two, [((HD, BLK), BF16)], (share, near(share, "zh")), smem=0, after=(dq,)
    )
    (done,) = call(sum_two, [((HD, BLK), BF16)], (near_sum, far(near_sum, "zh")), smem=0)
    done_far = over_pair(done)
    dq_far = lax.optimization_barrier((dq_far, near_sum))[0]
    dk_far, dv_near, _ = lax.optimization_barrier((dk_far, dv_near, done))

    dq, dq_near = call(sum_split, [((HD, BLK), BF16)] * 2, (dq, far(dq_far, "x")), smem=0)
    mixed, mixed_near = call(
        sum_split, [((32, 2048), BF16)] * 2, (mixed, far(mixed_far, "y")), smem=0, after=(done,)
    )
    mixed_other = near(mixed_near, "y")
    (stack,) = call(weight_stack, [((2 * HD, BLK), BF16)], (pos, done, done_far), after=(dq_near,))
    stacks = [stack, near(stack, "x"), far(stack, "x"), opposite(stack, "x")]
    dk, dk_near = call(
        sum_split, [((BLK, HD), BF16)] * 2, (dk, far(dk_far, "zh")), smem=0, after=(mixed_other,)
    )
    dv, dv_far = call(
        sum_split, [((BLK, HD), BF16)] * 2, (dv, near(dv_near, "zh")), smem=0
    )
    dq_near = lax.optimization_barrier((dq_near, stacks[1]))[0]
    out_keep, out_send = call(
        gather_grads,
        [((3 * TILE, HD), BF16)] * 2,
        (dk, near(dk_near, "zh"), dv, far(dv_far, "zh"), dq, near(dq_near, "x")),
        smem=0,
    )

    (here,) = call(
        weight_row, [((2 * HD, 1024), BF16)], (pos, *stacks), after=(out_send,)
    )
    out_recv = over_pair(out_send)
    grad_weight, mixed, written = call(
        weight_out,
        [((2 * HD, 2048), F32), ((32, 2048), BF16), ((8, HD), F32)],
        (pos, here, over_core(here), mixed, mixed_other),
        scratch=[
            pltpu.VMEM((2, 2 * HD, 1024), F32),
            pltpu.VMEM((32, 2048), BF16),
            pltpu.SemaphoreType.DMA((3,)),
        ],
        out_space=[pl.ANY, pl.ANY, pltpu.VMEM],
    )
    grad_q, grad_k, grad_v = call(
        join_heads,
        [((TILE, 2 * HD), BF16)] * 3,
        (pos, out_keep, out_recv),
        scratch=[pltpu.VMEM((3, TILE, 2 * HD), BF16), pltpu.SemaphoreType.DMA((3,))],
        out_space=pl.ANY,
        after=(written,),
    )
    return (mixed[None], grad_q[None], grad_k[None], grad_v[None], grad_weight)


def solution(mesh):
    mesh = Mesh(mesh.devices.reshape(4, 4, 2, 4, 2), AXES)
    tokens = ("x", "zh", "par")
    rows = P("core", tokens, "y")
    blocks = P("core", (*tokens, "y"), None)
    weight = P("y", None)
    return jax.shard_map(
        on_device,
        mesh=mesh,
        in_specs=(rows, rows, rows, weight, blocks, P()),
        out_specs=(blocks, rows, rows, rows, weight),
        check_vma=False,
    )
```
